32 devices in a mesh: row: 4 (over z), col: 8 (over y, x, core).
Axes of the slice: x: 2, y: 2, z: 4, core: 2. Of those that a mesh axis runs over, the one named last changes fastest.
Arguments:
- inputs: bfloat16 [2, 8192, 2048], P(None, 'row', 'col'), may hold values from -6 to 6
- cotangent: bfloat16 [2, 8192, 2048], P(None, 'row', 'col'), may hold values from -6 to 6
- segment: int32 [2, 8192], P(None, 'row'), may hold values from 0 to 31, never falling along the last dimension, each value on 1 to 800 neighbouring positions
- norm_gain: bfloat16 [2048], P(('col', 'row')), may hold values from 0.099609375 to 1.8984375
- w_query: bfloat16 [2048, 2048], P('row', 'col'), may hold values from -0.125 to 0.125
- w_key: bfloat16 [2048, 2048], P('row', 'col'), may hold values from -0.125 to 0.125
- w_value: bfloat16 [2048, 2048], P('row', 'col'), may hold values from -0.125 to 0.125
- w_beta: bfloat16 [2048, 16], P('row', 'col'), may hold values from -0.125 to 0.125
- conv_query: bfloat16 [2048, 4], P(('col', 'row')), may hold values from -3 to 3
- conv_key: bfloat16 [2048, 4], P(('col', 'row')), may hold values from -3 to 3
- conv_value: bfloat16 [2048, 4], P(('col', 'row')), may hold values from -3 to 3
- head_gain: bfloat16 [128], P('row'), may hold values from 0.099609375 to 1.8984375
- w_out: bfloat16 [2048, 2048], P('col', 'row'), may hold values from -0.125 to 0.125
- ffn_gain: bfloat16 [2048], P(('col', 'row')), may hold values from 0.099609375 to 1.8984375
- w_gate: bfloat16 [2048, 5632], P('row', 'col'), may hold values from -0.125 to 0.125
- w_up: bfloat16 [2048, 5632], P('row', 'col'), may hold values from -0.125 to 0.125
- w_down: bfloat16 [5632, 2048], P('col', 'row'), may hold values from -0.078125 to 0.078125
Outputs:
- output: bfloat16 [2, 8192, 2048], P(None, 'row', 'col')
- input_grad: float32 [2, 8192, 2048], P(None, 'row', 'col')
- grad_norm_gain: float32 [2048], P(('col', 'row'))
- grad_w_query: float32 [2048, 2048], P('row', 'col')
- grad_w_key: float32 [2048, 2048], P('row', 'col')
- grad_w_value: float32 [2048, 2048], P('row', 'col')
- grad_w_beta: float32 [2048, 16], P('row', 'col')
- grad_conv_query: float32 [2048, 4], P(('col', 'row'))
- grad_conv_key: float32 [2048, 4], P(('col', 'row'))
- grad_conv_value: float32 [2048, 4], P(('col', 'row'))
- grad_head_gain: float32 [128], P('row')
- grad_w_out: float32 [2048, 2048], P('col', 'row')
- grad_ffn_gain: float32 [2048], P(('col', 'row'))
- grad_w_gate: float32 [2048, 5632], P('row', 'col')
- grad_w_up: float32 [2048, 5632], P('row', 'col')
- grad_w_down: float32 [5632, 2048], P('col', 'row')
The draws below stay inside these ranges and needn't reach their ends.
Inputs may be any that keep to these rules, and one draw needn't show every extreme that they name: `segment`: along each micro-batch's 8192 tokens the numbers never fall, and each number covers 1 to 800 consecutive tokens.
All inputs are finite; a program needn't handle non-finite values.
Results may differ from the reference program's by a relative error of at most 0.014.
Values may be sent and summed in bfloat16 or wider, within the bound.
No kernel may reach another device: no remote copies, remote signals or barrier semaphores. Data moves between devices by JAX's collectives and lax.ppermute only.
A program may use at most 384 MiB of HBM per device.

```python
import math
import jax
import jax.numpy as jnp
import numpy as np
from jax import lax

D = 2048
H = 16
DK = 128
FF = 5632
CONV = 4
GROUP = 64
SEQ = 2048
MICRO = 2
TOKENS = 8192
SEGS = 32
MOST = 800


def steps_of(stream_key, dims, shards, least, high):
    level, own = 1.0, jax.random.fold_in(stream_key, 6)
    for position, shards_of in shards:
        steps = jnp.exp(jax.random.uniform(jax.random.fold_in(own, position), (shards_of,), jnp.float32, least / len(shards), high / len(shards)))
        level = level * jnp.repeat(steps, dims[position] // shards_of).reshape([-1 if axis == position else 1 for axis in range(len(dims))])
    return level


def length_profile(amount, total, most, skew):
    weights = [(1 << 20) // math.isqrt(rank ** skew) + 1 for rank in range(2, amount + 1)]
    surplus, counts = total - most - (amount - 1), [1] * (amount - 1)
    while surplus > 0:
        free = [i for i in range(amount - 1) if counts[i] < most]
        pool, budget = sum([weights[i] for i in free]), surplus
        for i in free:
            extra = min(most - counts[i], max(1, budget * weights[i] // pool), surplus)
            counts[i] = counts[i] + extra
            surplus = surplus - extra
    return np.array([most] + counts)


def uneven_parts(stream_key, number_of, total, reach, slope):
    if number_of == 2:
        one = jax.random.randint(stream_key, (), max(1, total - reach), min(reach, total - 1) + 1)
        return jnp.stack([one, total - one])
    lengths = jnp.asarray(length_profile(number_of, total, reach, slope), jnp.int32)
    couples = (number_of - 1) // 2
    giver, sink = lengths[1:1 + 2 * couples:2], lengths[2:2 + 2 * couples:2]
    room = jnp.minimum(giver - 1, reach - sink)
    passed = jax.random.randint(jax.random.fold_in(stream_key, 1), (couples,), 0, 1 << 20) % (room + 1)
    lengths = lengths.at[1:1 + 2 * couples:2].set(giver - passed).at[2:2 + 2 * couples:2].set(sink + passed)
    return lengths[jax.random.permutation(jax.random.fold_in(stream_key, 2), number_of)]


def scatter_about(key, extent, width, most, cuts=(), held_as=jnp.bfloat16):
    factor_of = steps_of(key, extent, cuts, -0.22, 0.18) if cuts else 1.0
    drawn = jax.random.normal(key, extent, jnp.float32) * width * factor_of
    return jnp.minimum(jnp.maximum(drawn, -most), most).astype(held_as)


def setup_inputs(seed: int = 0) -> dict:
    key_of = jax.random.split(jax.random.key(seed), 18)
    inputs = scatter_about(key_of[0], (MICRO, TOKENS, D), 1.0, 6.0, ((1, 4), (2, 8)))
    cotangent = scatter_about(key_of[1], (MICRO, TOKENS, D), 1.0, 6.0, ((1, 4), (2, 8)))
    segment = jax.vmap(lambda own: jnp.searchsorted(jnp.cumsum(uneven_parts(own, SEGS, TOKENS, MOST, 1)), jnp.arange(TOKENS), side="right"))(jax.random.split(key_of[2], MICRO)).reshape((MICRO, TOKENS)).astype(jnp.int32)
    norm_gain = jnp.clip(1.0 + 0.18 * jax.random.normal(key_of[3], (D,), jnp.float32), 0.099609375, 1.8984375).astype(jnp.bfloat16)
    w_query = scatter_about(key_of[4], (D, D), D ** -0.5, 0.125, ((0, 4), (1, 8)))
    w_key = scatter_about(key_of[5], (D, D), D ** -0.5, 0.125, ((0, 4), (1, 8)))
    w_value = scatter_about(key_of[6], (D, D), D ** -0.5, 0.125, ((0, 4), (1, 8)))
    w_beta = scatter_about(key_of[7], (D, H), D ** -0.5, 0.125, ((0, 4), (1, 8)))
    conv_query = scatter_about(key_of[8], (D, CONV), CONV ** -0.5, 3.0, ((0, 32),))
    conv_key = scatter_about(key_of[9], (D, CONV), CONV ** -0.5, 3.0, ((0, 32),))
    conv_value = scatter_about(key_of[10], (D, CONV), CONV ** -0.5, 3.0, ((0, 32),))
    head_gain = jnp.clip(1.0 + 0.18 * jax.random.normal(key_of[11], (DK,), jnp.float32), 0.099609375, 1.8984375).astype(jnp.bfloat16)
    w_out = scatter_about(key_of[12], (D, D), D ** -0.5, 0.125, ((0, 8), (1, 4)))
    ffn_gain = jnp.clip(1.0 + 0.18 * jax.random.normal(key_of[13], (D,), jnp.float32), 0.099609375, 1.8984375).astype(jnp.bfloat16)
    w_gate = scatter_about(key_of[14], (D, FF), D ** -0.5, 0.125, ((0, 4), (1, 8)))
    w_up = scatter_about(key_of[15], (D, FF), D ** -0.5, 0.125, ((0, 4), (1, 8)))
    w_down = scatter_about(key_of[16], (FF, D), FF ** -0.5, 0.078125, ((0, 8), (1, 4)))
    return dict(inputs=inputs, cotangent=cotangent, segment=segment, norm_gain=norm_gain, w_query=w_query, w_key=w_key, w_value=w_value, w_beta=w_beta, conv_query=conv_query, conv_key=conv_key, conv_value=conv_value, head_gain=head_gain, w_out=w_out, ffn_gain=ffn_gain, w_gate=w_gate, w_up=w_up, w_down=w_down)


EPSILON = 1e-06
HEAD_FLOOR = 0.002
HIGHEST = lax.Precision.HIGHEST

@jax.custom_vjp
def low(v):
    return lax.optimization_barrier(v.astype(jnp.bfloat16)).astype(jnp.float32)

@jax.custom_vjp
def low_back(v):
    return v

def low_keep(v):
    return (low(v), None)

def low_pass(kept, grad):
    return (grad,)

def back_keep(v):
    return (v, None)

def back_low(kept, grad):
    return (low(grad),)
low.defvjp(low_keep, low_pass)
low_back.defvjp(back_keep, back_low)

def matmul(left, right):
    return jnp.dot(left, right, precision=HIGHEST, preferred_element_type=left.dtype)

def rms_rows(values):
    return values * lax.rsqrt(lax.optimization_barrier(jnp.mean(values * values, axis=-1, keepdims=True)) + EPSILON)

def short_conv(pre_values, taps, labels):
    total = pre_values * taps[:, 0]
    for offset in range(1, CONV):
        shifted = jnp.concatenate([jnp.zeros((offset, pre_values.shape[1]), pre_values.dtype), pre_values[:-offset]], axis=0)
        earlier = jnp.concatenate([jnp.full((offset,), -1, jnp.int32), labels[:-offset]], axis=0)
        keep_mask = (earlier == labels).astype(pre_values.dtype)
        total = total + keep_mask[:, None] * shifted * taps[:, offset]
    return total

def delta_token(memory, items):
    query_t, key_t, value_t, beta_t, fresh_t = items
    prior = memory * (1.0 - fresh_t)
    wrong = value_t - jnp.einsum('hd,hde->he', key_t, prior, precision=HIGHEST)
    memory = prior + beta_t[:, None, None] * key_t[:, :, None] * wrong[:, None, :]
    return (memory, jnp.einsum('hd,hde->he', query_t, memory, precision=HIGHEST))

def delta_block(memory, items):
    return lax.scan(delta_token, memory, items)

def delta_rule(queries, keys, values, betas, fresh):
    blocks = SEQ // GROUP
    shaped = tuple((item.reshape((blocks, GROUP) + item.shape[1:]) for item in (queries, keys, values, betas, fresh)))
    start = jnp.zeros((H, DK, DK), queries.dtype)
    memory, outputs = lax.scan(jax.checkpoint(delta_block), start, shaped)
    return outputs.reshape(SEQ, H, DK)

def layer(params, inputs, labels):
    gain_one, query_w, key_w, value_w, beta_w, conv_q, conv_k, conv_v, gain_head, out_w, gain_two, gate_w, up_w, down_w = params
    act_one = low(rms_rows(inputs) * gain_one)
    query_pre = low_back(matmul(act_one, query_w))
    key_pre = low_back(matmul(act_one, key_w))
    value_pre = low_back(matmul(act_one, value_w))
    beta_pre = low_back(matmul(act_one, beta_w))
    query_act = jax.nn.silu(short_conv(query_pre, conv_q, labels)).reshape(SEQ, H, DK)
    key_act = jax.nn.silu(short_conv(key_pre, conv_k, labels)).reshape(SEQ, H, DK)
    value_act = jax.nn.silu(short_conv(value_pre, conv_v, labels)).reshape(SEQ, H, DK)
    query_unit = query_act * lax.rsqrt(lax.optimization_barrier(jnp.sum(query_act * query_act, axis=-1, keepdims=True)) + EPSILON) * DK ** (-0.5)
    key_unit = key_act * lax.rsqrt(lax.optimization_barrier(jnp.sum(key_act * key_act, axis=-1, keepdims=True)) + EPSILON)
    betas = jax.nn.sigmoid(beta_pre)
    earlier = jnp.concatenate([jnp.full((1,), -1, jnp.int32), labels[:-1]], axis=0)
    fresh = (earlier != labels).astype(query_unit.dtype)
    mixed = delta_rule(query_unit, key_unit, value_act, betas, fresh)
    head_scale = lax.rsqrt(jnp.maximum(lax.optimization_barrier(jnp.mean(mixed * mixed, axis=-1, keepdims=True)), HEAD_FLOOR))
    head_out = low((mixed * head_scale * gain_head).reshape(SEQ, D))
    resid = inputs + low_back(matmul(head_out, out_w))
    act_two = low(rms_rows(resid) * gain_two)
    gate_pre = low_back(matmul(act_two, gate_w))
    up_pre = low_back(matmul(act_two, up_w))
    hidden = low(jax.nn.silu(gate_pre) * up_pre)
    return resid + low_back(matmul(hidden, down_w))

def reference(inputs, cotangent, segment, norm_gain, w_query, w_key, w_value, w_beta, conv_query, conv_key, conv_value, head_gain, w_out, ffn_gain, w_gate, w_up, w_down):
    weights = tuple((weight_in.astype(jnp.float32) for weight_in in (norm_gain, w_query, w_key, w_value, w_beta, conv_query, conv_key, conv_value, head_gain, w_out, ffn_gain, w_gate, w_up, w_down)))
    seq_count = MICRO * TOKENS // SEQ
    flat_in = inputs.astype(jnp.float32).reshape(seq_count, SEQ, D)
    flat_seg = segment.astype(jnp.int32).reshape(seq_count, SEQ)
    flat_cot = cotangent.astype(jnp.float32).reshape(seq_count, SEQ, D)
    checked = jax.checkpoint(layer)

    def forward(params, values):

        def one_sequence(items):
            return checked(params, items[0], items[1])
        return lax.map(one_sequence, (values, flat_seg))
    result, backward = jax.vjp(forward, weights, flat_in)
    grads, input_grad = backward(flat_cot)
    shape_out = (MICRO, TOKENS, D)
    return (result.astype(jnp.bfloat16).reshape(shape_out), input_grad.reshape(shape_out), grads[0], grads[1], grads[2], grads[3], grads[4], grads[5], grads[6], grads[7], grads[8], grads[9], grads[10], grads[11], grads[12], grads[13])
```

```python
from functools import partial

import jax
import jax.numpy as jnp
from jax import lax
from jax.experimental import pallas as pl
from jax.experimental.pallas import tpu as pltpu
from jax.sharding import PartitionSpec as P

SEQ = 2048
CHUNK = 128
FWD_SUB = 4
BWD_SUB = 2
TILE = 512
HALO = 8
EPSILON = 1e-06
HEAD_FLOOR = 0.002
BF = jnp.bfloat16
F32 = jnp.float32
FFN_TILE = 256
PER_MICRO = 4.0e8


def dot_nn(a, b):
    return lax.dot_general(a, b, (((1,), (0,)), ((), ())), preferred_element_type=F32)


def dot_nt(a, b):
    return lax.dot_general(a, b, (((1,), (1,)), ((), ())), preferred_element_type=F32)


def dot_tn(a, b):
    return lax.dot_general(a, b, (((0,), (0,)), ((), ())), preferred_element_type=F32)


def token_marks(labels, chunk):
    seqs, length = labels.shape
    padded_back = jnp.pad(labels, ((0, 0), (4, 0)), constant_values=-1)
    padded_fore = jnp.pad(labels, ((0, 0), (0, 4)), constant_values=-2)
    marks = [labels]
    for lag in (1, 2, 3):
        marks.append(padded_back[:, 4 - lag : 4 - lag + length] == labels)
    for lag in (1, 2, 3):
        marks.append(padded_fore[:, lag : lag + length] == labels)
    grid = labels.reshape(seqs, length // chunk, chunk)
    prior = jnp.pad(grid[:, :-1, -1], ((0, 0), (1, 0)), constant_values=-1)
    marks.append((grid == prior[:, :, None]).reshape(seqs, length))
    marks.append((grid == grid[:, :, -1:]).reshape(seqs, length))
    marks.append(
        jnp.broadcast_to((grid[:, :, -1] == prior)[:, :, None], grid.shape).reshape(seqs, length)
    )
    marks += [jnp.zeros_like(labels)] * (16 - len(marks))
    marks = [mark.astype(F32).reshape(seqs, length // chunk, 1, chunk) for mark in marks]
    return jnp.concatenate(marks, axis=2)


LABEL, BACK, FORE, CARRIED, LAST, KEEP = 0, 0, 3, 7, 8, 9


def sigmoid(x):
    return 1.0 / (1.0 + jnp.exp(-x))


def level_marks(size):
    row = lax.broadcasted_iota(jnp.int32, (size, size), 0)
    col = lax.broadcasted_iota(jnp.int32, (size, size), 1)
    return row == col, row ^ col


def unit_lower_inverses(systems):
    size = systems[0].shape[0]
    diagonal, differ = level_marks(size)
    inverses = [
        (jnp.where(diagonal, 1.0, 0.0) - jnp.where(differ == 1, system, 0.0)).astype(BF)
        for system in systems
    ]
    block = 2
    while block < size:
        level = (differ >= block) & (differ < 2 * block)
        offs = [jnp.where(level, system, 0.0).astype(BF) for system in systems]
        lefts = [dot_nn(inverse, off).astype(BF) for inverse, off in zip(inverses, offs)]
        inverses = [
            inverse - dot_nn(left, inverse).astype(BF) for inverse, left in zip(inverses, lefts)
        ]
        block *= 2
    return inverses


def conv_rows(ext, taps, marks, lane, first, chunk):
    here = ext[pl.ds(HALO + first, chunk), lane]
    shifted = [here]
    total = here * taps[0:1, lane]
    for lag in (1, 2, 3):
        moved = ext[pl.ds(HALO + first - lag, chunk), lane] * marks[:, BACK + lag : BACK + lag + 1]
        shifted.append(moved)
        total = total + moved * taps[lag : lag + 1, lane]
    return total, shifted


def chunk_marks(marks_ref, seq, part, chunk):
    by_row = marks_ref[seq, part]
    marks = jnp.transpose(by_row)
    row = lax.broadcasted_iota(jnp.int32, (chunk, chunk), 0)
    col = lax.broadcasted_iota(jnp.int32, (chunk, chunk), 1)
    same = marks[:, LABEL : LABEL + 1] == by_row[LABEL : LABEL + 1, :]
    return (
        marks,
        same & (row > col),
        same & (row >= col),
        marks[:, CARRIED : CARRIED + 1],
        marks[:, LAST : LAST + 1],
        marks[0:1, KEEP : KEEP + 1],
    )


def mix_fwd_kernel(
    heads, chunk, sub, marks_ref, taps_ref, gain_ref, pre_ref,
    ao_ref, o_ref, u_ref, w_ref, state_ref, inv_ref, ext, memory,
):
    seqs = pre_ref.shape[0]
    wide = 3 * heads * 128
    size = sub * chunk

    @pl.when(pl.program_id(0) == 0)
    def _():
        ext[:, 0:HALO, :] = jnp.zeros((seqs, HALO, wide), F32)
        memory[...] = jnp.zeros_like(memory)

    ext[:, HALO : HALO + size, :] = pre_ref[:, :, 0:wide]
    kept = {
        (seq, part): chunk_marks(marks_ref, seq, part, chunk)
        for seq in range(seqs)
        for part in range(sub)
    }
    chains = [(seq, head) for seq in range(seqs) for head in range(heads)]
    units = [(seq, head, part) for part in range(sub) for seq, head in chains]
    boths, values, betas, attns, keys_list, systems = {}, {}, {}, {}, {}, {}
    for unit in units:
        seq, head, part = unit
        marks = kept[seq, part][0]
        acts = []
        for kind in range(3):
            lane = pl.ds((kind * heads + head) * 128, 128)
            cv, _ = conv_rows(ext.at[seq], taps_ref, marks, lane, part * chunk, chunk)
            acts.append(cv * sigmoid(cv))
        q1, k1, values[unit] = acts
        qn = q1 * (lax.rsqrt(jnp.sum(q1 * q1, axis=1, keepdims=True) + EPSILON) * 128 ** (-0.5))
        kn = k1 * lax.rsqrt(jnp.sum(k1 * k1, axis=1, keepdims=True) + EPSILON)
        betas[unit] = sigmoid(
            pre_ref[seq, part * chunk : (part + 1) * chunk, wide + head : wide + head + 1]
        )
        boths[unit] = jnp.concatenate([qn.astype(BF), kn.astype(BF)], axis=0)
    for unit in units:
        _, strict, within, _, _, _ = kept[unit[0], unit[2]]
        scores = dot_nt(boths[unit], boths[unit][chunk:])
        attns[unit] = jnp.where(within, scores[:chunk], 0.0).astype(BF)
        keys = jnp.where(strict, scores[chunk:], 0.0)
        keys_list[unit] = keys.astype(BF)
        systems[unit] = keys * betas[unit]
    inverses = dict(zip(units, unit_lower_inverses([systems[unit] for unit in units])))
    for part in range(sub):
        here = [(seq, head, part) for seq, head in chains]
        states = [memory[index] for index in range(len(here))]
        lows = [state.astype(BF) for state in states]
        seens = [dot_nn(boths[unit], low) for unit, low in zip(here, lows)]
        rights = [
            values[unit] - kept[unit[0], part][3] * seen[chunk:]
            for unit, seen in zip(here, seens)
        ]
        updates = [
            dot_nn(inverses[unit], (betas[unit] * right).astype(BF))
            for unit, right in zip(here, rights)
        ]
        for index, unit in enumerate(here):
            last, keep = kept[unit[0], part][4:]
            memory[index] = keep * states[index] + dot_tn(
                boths[unit][chunk:], (last * updates[index]).astype(BF)
            )
        for index, unit in enumerate(here):
            seq, head, _ = unit
            carried = kept[seq, part][3]
            rows = slice(part * chunk, (part + 1) * chunk)
            ub = updates[index].astype(BF)
            mixed = dot_nn(jnp.concatenate([attns[unit], keys_list[unit]], axis=0), ub)
            out = carried * seens[index][:chunk] + mixed[:chunk]
            wrong = rights[index] - mixed[chunk:]
            lane = pl.ds(head * 128, 128)
            scale = lax.rsqrt(jnp.maximum(jnp.mean(out * out, axis=1, keepdims=True), HEAD_FLOOR))
            ao_ref[seq, rows, lane] = (out * scale * gain_ref[...]).astype(BF)
            o_ref[seq, rows, lane] = out
            u_ref[seq, rows, lane] = ub
            w_ref[seq, rows, lane] = wrong.astype(BF)
            inv_ref[part, index] = inverses[unit]
            state_ref[part, index] = lows[index]
    ext[:, 0:HALO, :] = ext[:, size : size + HALO, :]


def mix_bwd_kernel(
    heads, chunk, sub, marks_ref, taps_ref, gain_ref,
    o_ref, u_ref, w_ref, state_ref, inv_ref, pre_ref, halo_ref, dao_ref,
    dpre_ref, stat_ref, dconv_ref, dgain_ref, ext, dext, memory,
):
    seqs = pre_ref.shape[0]
    wide = 3 * heads * 128
    size = sub * chunk

    @pl.when(pl.program_id(0) == 0)
    def _():
        dext[:, size : size + HALO, :] = jnp.zeros((seqs, HALO, wide), F32)
        memory[...] = jnp.zeros_like(memory)
        dconv_ref[...] = jnp.zeros_like(dconv_ref)
        dgain_ref[...] = jnp.zeros_like(dgain_ref)

    ext[:, 0:HALO, :] = halo_ref[:, :, 0:wide]
    ext[:, HALO : HALO + size, :] = pre_ref[:, :, 0:wide]
    gain = gain_ref[...]

    def fold(rows):
        return jnp.sum(rows.reshape(chunk // 8, 8, 128), axis=0)

    kept = {
        (seq, part): chunk_marks(marks_ref, seq, part, chunk)
        for seq in range(seqs)
        for part in range(sub)
    }
    chains = [(seq, head) for seq in range(seqs) for head in range(heads)]
    units = [(seq, head, part) for part in reversed(range(sub)) for seq, head in chains]

    def rows_of(unit):
        return slice(unit[2] * chunk, (unit[2] + 1) * chunk)

    def lane_of(unit, kind=0):
        return pl.ds((kind * heads + unit[1]) * 128, 128)

    acts, scales, norms, betas, boths, dobs, cdos = {}, {}, {}, {}, {}, {}, {}
    for unit in units:
        seq, head, part = unit
        marks, _, _, carried, _, _ = kept[seq, part]
        for kind in range(3):
            cv, _ = conv_rows(
                ext.at[seq], taps_ref, marks, lane_of(unit, kind), part * chunk, chunk
            )
            sg = sigmoid(cv)
            acts[unit, kind] = cv * sg
            scales[unit, kind] = sg * (1.0 + cv * (1.0 - sg))
        q1, k1 = acts[unit, 0], acts[unit, 1]
        rq = lax.rsqrt(jnp.sum(q1 * q1, axis=1, keepdims=True) + EPSILON)
        rk = lax.rsqrt(jnp.sum(k1 * k1, axis=1, keepdims=True) + EPSILON)
        norms[unit] = rq, rk
        boths[unit] = jnp.concatenate(
            [(q1 * (rq * 128 ** (-0.5))).astype(BF), (k1 * rk).astype(BF)], axis=0
        )
        betas[unit] = sigmoid(pre_ref[seq, rows_of(unit), wide + head : wide + head + 1])
        out = o_ref[seq, rows_of(unit), lane_of(unit)]
        square = jnp.mean(out * out, axis=1, keepdims=True)
        scale = lax.rsqrt(jnp.maximum(square, HEAD_FLOOR))
        ro = out * scale
        dao = dao_ref[seq, rows_of(unit), lane_of(unit)]
        dgain_ref[...] += fold(dao * ro)
        eo = dao * gain
        inner = jnp.mean(eo * ro, axis=1, keepdims=True)
        inner = jnp.where(square > HEAD_FLOOR, inner, 0.0)
        do = scale * (eo - ro * inner)
        dobs[unit] = do.astype(BF)
        cdos[unit] = (carried * do).astype(BF)
    firsts, grows, crosses = {}, {}, {}
    for unit in units:
        _, _, within, _, _, _ = kept[unit[0], unit[2]]
        both = boths[unit]
        attn = jnp.where(within, dot_nt(both[:chunk], both[chunk:]), 0.0).astype(BF)
        firsts[unit] = dot_tn(attn, dobs[unit])
        grows[unit] = dot_tn(both[:chunk], cdos[unit])
    drs, seconds, dbetas = {}, {}, {}
    for part in reversed(range(sub)):
        here = [(seq, head, part) for seq, head in chains]
        olds = [memory[index] for index in range(len(here))]
        lows = [old.astype(BF) for old in olds]
        fromstate = [dot_nn(boths[unit][chunk:], low) for unit, low in zip(here, lows)]
        dus = [
            (firsts[unit] + kept[unit[0], part][4] * term).astype(BF)
            for unit, term in zip(here, fromstate)
        ]
        drhs = [dot_tn(inv_ref[part, index], du) for index, du in enumerate(dus)]
        for index, unit in enumerate(here):
            drs[unit] = betas[unit] * drhs[index]
            carried, _, keep = kept[unit[0], part][3:]
            memory[index] = (
                keep * olds[index]
                + grows[unit]
                - dot_tn(boths[unit][chunk:], (carried * drs[unit]).astype(BF))
            )
        for index, unit in enumerate(here):
            wrong = w_ref[unit[0], rows_of(unit), lane_of(unit)].astype(F32)
            dbetas[unit] = jnp.sum(drhs[index] * wrong, axis=1, keepdims=True)
            seconds[unit] = dot_nt(u_ref[unit[0], rows_of(unit), lane_of(unit)], lows[index])
    shares = {}
    for unit in units:
        seq, head, part = unit
        marks, strict, within, carried, last, _ = kept[seq, part]
        both, kb = boths[unit], boths[unit][chunk:]
        index = seq * heads + head
        stack = jnp.concatenate([dobs[unit], drs[unit].astype(BF)], axis=0)
        right = jnp.concatenate(
            [u_ref[seq, rows_of(unit), lane_of(unit)], state_ref[part, index]], axis=0
        )
        cross = dot_nt(stack, right)
        dattn = jnp.where(within, cross[:chunk, :chunk], 0.0).astype(BF)
        dkeys = jnp.where(strict, -cross[chunk:, :chunk], 0.0).astype(BF)
        dboth = jnp.concatenate([dattn, dkeys], axis=0)
        by_row = dot_nn(dboth, kb)
        dqn = carried * cross[:chunk, chunk:] + by_row[:chunk]
        dkn = (
            dot_tn(dboth, both)
            + last * seconds[unit]
            + by_row[chunk:]
            - carried * cross[chunk:, chunk:]
        )
        (rq, rk), q1, k1 = norms[unit], acts[unit, 0], acts[unit, 1]
        dq1 = 128 ** (-0.5) * rq * (
            dqn - (rq * rq) * q1 * jnp.sum(q1 * dqn, axis=1, keepdims=True)
        )
        dk1 = rk * (dkn - (rk * rk) * k1 * jnp.sum(k1 * dkn, axis=1, keepdims=True))
        for kind, dact in enumerate((dq1, dk1, drs[unit])):
            dext[seq, rows_of(unit), lane_of(unit, kind)] = dact * scales[unit, kind]
    for unit in units:
        seq, head, part = unit
        marks = kept[seq, part][0]
        share = shares.get((seq, part), 0.0)
        for kind in range(3):
            lane = lane_of(unit, kind)
            _, shifts = conv_rows(ext.at[seq], taps_ref, marks, lane, part * chunk, chunk)
            dc = dext[seq, rows_of(unit), lane]
            back = dc * taps_ref[0:1, lane]
            dconv_ref[0:8, lane] += fold(dc * shifts[0])
            for lag in (1, 2, 3):
                dconv_ref[8 * lag : 8 * lag + 8, lane] += fold(dc * shifts[lag])
                back = back + (
                    dext[seq, pl.ds(part * chunk + lag, chunk), lane]
                    * marks[:, FORE + lag : FORE + lag + 1]
                    * taps_ref[lag : lag + 1, lane]
                )
            dpre_ref[seq, rows_of(unit), lane] = back.astype(BF)
            share = share + back * shifts[0]
        shares[seq, part] = share
    column = lax.broadcasted_iota(jnp.int32, (chunk, 128), 1)
    for seq, part in kept:
        rows = slice(part * chunk, (part + 1) * chunk)
        total = jnp.zeros((chunk, 128), F32)
        for head in range(heads):
            unit = seq, head, part
            grad = dbetas[unit] * betas[unit] * (1.0 - betas[unit])
            total = jnp.where(column == head, grad, total)
        dpre_ref[seq, rows, pl.ds(wide, 128)] = total.astype(BF)
        share = shares[seq, part] + total * pre_ref[seq, rows, pl.ds(wide, 128)]
        stat_ref[seq, rows] = jnp.broadcast_to(
            jnp.sum(share, axis=1, keepdims=True), (chunk, 128)
        )
    dext[:, size : size + HALO, :] = dext[:, 0:HALO, :]


def params():
    return pltpu.CompilerParams(dimension_semantics=("arbitrary",), vmem_limit_bytes=60 * 2**20)


def fixed(array):
    zeros = (0,) * array.ndim
    return pl.BlockSpec(array.shape, lambda n: zeros, pipeline_mode=pl.Buffered(1))


def cost(micros):
    return pl.CostEstimate(flops=int(micros * PER_MICRO), bytes_accessed=0, transcendentals=0)


def shape(dims, dtype):
    return jax.ShapeDtypeStruct(dims, dtype)


def mix_forward(pre, marks, taps, gain, heads, chunk=CHUNK, sub=FWD_SUB):
    seqs, length, cols = pre.shape
    chains, parts = seqs * heads, length // chunk
    steps = parts // sub
    wide, hw = 3 * heads * 128, heads * 128

    def tok(width):
        return pl.BlockSpec((seqs, sub * chunk, width), lambda n: (0, n, 0))

    out_shape = [
        shape((seqs, length, hw), BF),
        shape((seqs, length, hw), F32),
        shape((seqs, length, hw), BF),
        shape((seqs, length, hw), BF),
        shape((parts, chains, 128, 128), BF),
        shape((parts, chains, chunk, chunk), BF),
    ]
    mixed, *saved = pl.pallas_call(
        partial(mix_fwd_kernel, heads, chunk, sub),
        grid=(steps,),
        in_specs=[
            pl.BlockSpec((seqs, sub, 16, chunk), lambda n: (0, n, 0, 0)),
            fixed(taps), fixed(gain), tok(cols),
        ],
        out_specs=[tok(hw)] * 4 + [
            pl.BlockSpec((sub, chains, 128, 128), lambda n: (n, 0, 0, 0)),
            pl.BlockSpec((sub, chains, chunk, chunk), lambda n: (n, 0, 0, 0)),
        ],
        out_shape=out_shape,
        scratch_shapes=[
            pltpu.VMEM((seqs, HALO + sub * chunk, wide), F32),
            pltpu.VMEM((chains, 128, 128), F32),
        ],
        compiler_params=params(),
        cost_estimate=cost(24),
        name="mix_forward",
    )(marks, taps, gain, pre)
    return mixed, saved


def mix_backward(pre, marks, taps, gain, saved, dao, heads, chunk=CHUNK, sub=BWD_SUB):
    seqs, length, cols = pre.shape
    chains, parts = seqs * heads, length // chunk
    steps = parts // sub
    wide, hw = 3 * heads * 128, heads * 128
    end, groups = steps - 1, sub * chunk // HALO

    def tok(width):
        return pl.BlockSpec((seqs, sub * chunk, width), lambda n: (0, end - n, 0))

    halo = pl.BlockSpec(
        (seqs, HALO, cols), lambda n: (0, jnp.maximum((end - n) * groups - 1, 0), 0)
    )
    out_shape = [
        shape((seqs, length, cols), BF), shape((seqs, length, 128), F32),
        shape((32, wide), F32), shape((8, 128), F32),
    ]
    return pl.pallas_call(
        partial(mix_bwd_kernel, heads, chunk, sub),
        grid=(steps,),
        in_specs=[
            pl.BlockSpec((seqs, sub, 16, chunk), lambda n: (0, end - n, 0, 0)),
            fixed(taps), fixed(gain),
        ] + [tok(hw)] * 3 + [
            pl.BlockSpec((sub, chains, 128, 128), lambda n: (end - n, 0, 0, 0)),
            pl.BlockSpec((sub, chains, chunk, chunk), lambda n: (end - n, 0, 0, 0)),
            tok(cols), halo, tok(hw),
        ],
        out_specs=[
            tok(cols), tok(128),
            pl.BlockSpec((32, wide), lambda n: (0, 0)),
            pl.BlockSpec((8, 128), lambda n: (0, 0)),
        ],
        out_shape=out_shape,
        scratch_shapes=[
            pltpu.VMEM((seqs, HALO + sub * chunk, wide), F32),
            pltpu.VMEM((seqs, HALO + sub * chunk, wide), F32),
            pltpu.VMEM((chains, 128, 128), F32),
        ],
        compiler_params=params(),
        cost_estimate=cost(34),
        name="mix_backward",
    )(marks, taps, gain, *saved, pre, pre, dao)


def swap(values, bit, ways):
    return lax.ppermute(values, "col", [(i, i ^ bit) for i in range(ways)])


def gather_cols(values, ways, way="direct"):
    base = [(0, 0, values)]
    if ways == 8:
        half = values.shape[-1] // 2
        along, across = swap(values, 2, ways), swap(values, 4, ways)
        base += [(2, 0, along), (4, 0, across)]
        if way == "direct":
            base.append((6, 0, swap(values, 6, ways)))
        elif way == "along":
            base.append((6, 0, swap(across, 2, ways)))
        elif way == "across":
            base.append((6, 0, swap(along, 4, ways)))
        else:
            base += [
                (6, 0, swap(across[..., :half], 2, ways)),
                (6, half, swap(along[..., half:], 4, ways)),
            ]
    else:
        bit = 2
        while bit < ways:
            base += [(far ^ bit, lane, swap(array, bit, ways)) for far, lane, array in base]
            bit *= 2
    return base


def other_core(base, ways):
    return base + [(far ^ 1, lane, swap(array, 1, ways)) for far, lane, array in base]


def after(values, *others):
    return lax.optimization_barrier((values, others))[0]


def arrays_of(pieces):
    return [array for _, _, array in pieces]


def pieces_after(pieces, *others):
    arrays = after(arrays_of(pieces), *others)
    return [(far, lane, array) for (far, lane, _), array in zip(pieces, arrays)]


def covered(results, pieces):
    results, arrays = lax.optimization_barrier((results, arrays_of(pieces)))
    return results, [(far, lane, array) for (far, lane, _), array in zip(pieces, arrays)]


def add_low(*terms):
    return sum(term.astype(F32) for term in terms).astype(BF)


def send_pairs(pieces, ways):
    return [(far, 0, swap(pieces[far | 1], 1, ways)) for far in range(0, ways, 2)]


def add_pairs(pieces, arrived):
    sums = [(far, 0, add_low(pieces[far], array)) for far, _, array in arrived if far]
    return (pieces[0], arrived[0][2]), sums


def scatter_cols(sums, ways, way="direct"):
    held = {far: array for far, _, array in sums}
    if ways == 8 and way == "direct":
        return [(far, 0, swap(held[far], far, ways)) for far in (2, 4, 6)]
    if ways == 8:
        half = held[2].shape[-1] // 2
        left = swap(held[6][..., :half], 2, ways)
        right = swap(held[6][..., half:], 4, ways)
        four = jnp.concatenate(
            [add_low(left, held[4][..., :half]), held[4][..., half:]], axis=-1
        )
        two = jnp.concatenate(
            [held[2][..., :half], add_low(right, held[2][..., half:])], axis=-1
        )
        return [(2, 0, swap(two, 2, ways)), (4, 0, swap(four, 4, ways))]
    terms = {far: (array,) for far, array in held.items()}
    terms[0] = ()
    bit = 2
    while bit < ways:
        terms = {
            far: terms[far] + (swap(add_low(*terms[far | bit]), bit, ways),)
            for far in terms
            if not far & bit
        }
        bit *= 2
    return [(0, 0, array) for array in terms[0]]


def total_of(own, arrived):
    return sum(array.astype(F32) for array in (*own, *arrays_of(arrived)))


def sum_over(values, axis, ways, bit=1, size=None):
    size = ways if size is None else size
    while bit < ways:
        values = values + lax.ppermute(values, axis, [(i, i ^ bit) for i in range(size)])
        bit *= 2
    return values


def place(spot_ref, layout, block):
    return [
        pl.multiple_of((spot_ref[0] ^ far) * block + lane, 128 if block % 128 == 0 else 1)
        for far, lane in layout
    ]


def norm_into(pieces, starts, gain_ref, act_ref):
    width = act_ref.shape[1]
    total = 0.0
    for piece in pieces:
        rows = piece[...].astype(F32)
        total = total + jnp.sum(rows * rows, axis=1, keepdims=True)
    inverse = lax.rsqrt(total / width + EPSILON)
    for start, piece in zip(starts, pieces):
        lanes = pl.ds(start, piece.shape[1])
        act_ref[:, lanes] = (piece[...].astype(F32) * inverse * gain_ref[0:1, lanes]).astype(BF)
    return inverse


def project_kernel(layout, block, spot_ref, gain_ref, weight_ref, *refs):
    count = len(layout)
    pieces, (pre_ref, act_ref, stat_ref) = refs[:count], refs[count:]
    starts = place(spot_ref, layout, block)
    inverse = norm_into(pieces, starts, gain_ref, act_ref)
    stat_ref[...] = jnp.broadcast_to(inverse, stat_ref.shape)
    pre_ref[...] = dot_nn(act_ref[...], weight_ref[...])


def spread_kernel(transposed, layout, block, spot_ref, weight_ref, rows_ref, *refs):
    outs, whole = refs[: len(layout)], refs[-1]
    parts, step = weight_ref.shape[0], whole.shape[1] // weight_ref.shape[0]
    rows = rows_ref[...]
    for part in range(parts):
        product = (dot_nt if transposed else dot_nn)(rows, weight_ref[part])
        whole[:, part * step : (part + 1) * step] = product.astype(BF)
    for start, out in zip(place(spot_ref, layout, block), outs):
        out[...] = whole[:, pl.ds(start, block)]


def collect_kernel(layout, block, spot_ref, weight_ref, *refs):
    count = len(layout)
    pieces, (whole_ref, out_ref) = refs[:count], refs[count:]
    for start, piece in zip(place(spot_ref, layout, block), pieces):
        whole_ref[:, pl.ds(start, piece.shape[1])] = piece[...]
    parts = weight_ref.shape[0]
    step = whole_ref.shape[1] // parts
    total = 0.0
    for part in range(parts):
        total = total + dot_nt(
            whole_ref[:, part * step : (part + 1) * step], weight_ref[part]
        )
    out_ref[...] = total


def ffn_kernel(layout, cot_layout, block, ways, spot_ref, gain_ref, gates_ref, ups_ref, down_ref, *refs):
    count, total = len(layout), len(layout) + len(cot_layout)
    acts, cots, refs = refs[:count], refs[count:total], refs[total:]
    act_ref, cot_ref, hid_ref, dgate_ref, dup_ref, stat_ref = refs[:6]
    grads, outs, whole = refs[6 : 6 + ways], refs[6 + ways : 6 + 2 * ways], refs[-1]
    starts = place(spot_ref, layout, block)
    inverse = norm_into(acts, starts, gain_ref, act_ref)
    for start, piece in zip(place(spot_ref, cot_layout, block), cots):
        cot_ref[:, pl.ds(start, piece.shape[1])] = piece[...]
    parts = gates_ref.shape[0]
    step = act_ref.shape[1] // parts
    gate, up, dhid = 0.0, 0.0, 0.0
    for part in range(parts):
        lanes = pl.ds(part * step, step)
        gate = gate + dot_nt(act_ref[:, lanes], gates_ref[part])
        up = up + dot_nt(act_ref[:, lanes], ups_ref[part])
        dhid = dhid + dot_nt(cot_ref[:, lanes], down_ref[part])
    sig = sigmoid(gate)
    swish = gate * sig
    hid = (swish * up).astype(BF)
    dgate = (dhid * up * sig * (1.0 + gate * (1.0 - sig))).astype(BF)
    dup = (dhid * swish).astype(BF)
    hid_ref[...] = hid
    dgate_ref[...] = dgate
    dup_ref[...] = dup
    inner = jnp.sum(dgate.astype(F32) * gate + dup.astype(F32) * up, axis=1, keepdims=True)
    lane = lax.broadcasted_iota(jnp.int32, stat_ref.shape, 1)
    stat_ref[...] = jnp.where(lane == 0, inverse, inner)
    spots = place(spot_ref, [(far, 0) for far in range(ways)], block)
    for part in range(parts):
        product = dot_nn(dgate, gates_ref[part]) + dot_nn(dup, ups_ref[part])
        whole[:, part * step : (part + 1) * step] = product.astype(BF)
    for start, out in zip(spots, grads):
        out[...] = whole[:, pl.ds(start, block)]
    for part in range(parts):
        whole[:, part * step : (part + 1) * step] = dot_nn(hid, down_ref[part]).astype(BF)
    for start, out in zip(spots, outs):
        out[...] = whole[:, pl.ds(start, block)]


SPOT = pl.BlockSpec(memory_space=pltpu.SMEM)


def rows_spec(width, tile):
    return pl.BlockSpec((tile, width), lambda n: (n, 0))


def tiled(kernel, name, fixed_args, row_args, out_shape, tile, micros, spot, scratch=()):
    rows = row_args[0].shape[0]
    return pl.pallas_call(
        kernel,
        grid=(rows // tile,),
        in_specs=[SPOT]
        + [fixed(a) for a in fixed_args]
        + [rows_spec(a.shape[1], tile) for a in row_args],
        out_specs=[rows_spec(a.shape[1], tile) for a in out_shape],
        out_shape=out_shape,
        scratch_shapes=list(scratch),
        compiler_params=params(),
        cost_estimate=cost(micros),
        name=name,
    )(spot, *fixed_args, *row_args)


def layout_of(pieces):
    return tuple((far, lane) for far, lane, _ in pieces), [array for _, _, array in pieces]


def project(pieces, gain, weight, spot, block):
    layout, arrays = layout_of(pieces)
    rows, (width, cols) = arrays[0].shape[0], weight.shape
    out = [shape((rows, cols), F32), shape((rows, width), BF), shape((rows, 128), F32)]
    return tiled(
        partial(project_kernel, layout, block), "project", [gain, weight], arrays, out,
        TILE, 19, spot,
    )


def spread(rows_in, weight, spot, block, ways, transposed):
    rows = rows_in.shape[0]
    width = block * ways
    layout = tuple((far, 0) for far in range(ways))
    return tiled(
        partial(spread_kernel, transposed, layout, block), "spread", [weight], [rows_in],
        [shape((rows, block), BF)] * ways, TILE, 14 if transposed else 7, spot,
        [pltpu.VMEM((TILE, width), BF)],
    )


def collect(pieces, weight, spot, block, ways):
    layout, arrays = layout_of(pieces)
    rows = arrays[0].shape[0]
    out = [shape((rows, block * ways), BF), shape((rows, weight.shape[1]), F32)]
    return tiled(
        partial(collect_kernel, layout, block), "collect", [weight], arrays, out,
        TILE, 9, spot,
    )


def feed_forward(acts, cots, gain, gates, ups, down, spot, block, ways):
    layout, act_arrays = layout_of(acts)
    cot_layout, cot_arrays = layout_of(cots)
    rows, width, hidden = act_arrays[0].shape[0], block * ways, down.shape[1]
    out = (
        [shape((rows, width), BF)] * 2
        + [shape((rows, hidden), BF)] * 3
        + [shape((rows, 128), F32)]
        + [shape((rows, block), BF)] * (2 * ways)
    )
    results = tiled(
        partial(ffn_kernel, layout, cot_layout, block, ways), "feed_forward", [gain, gates, ups, down],
        act_arrays + cot_arrays, out, FFN_TILE, 58, spot,
        [pltpu.VMEM((FFN_TILE, width), BF)],
    )
    return results[:6], results[6 : 6 + ways], results[6 + ways :]


def outer(lefts, rights):
    total = None
    for left, right in zip(lefts, rights):
        term = dot_tn(left, right)
        total = term if total is None else total + term
    return total


def scatter_row(values, dim):
    return lax.psum_scatter(
        values.astype(BF), "row", scatter_dimension=dim, tiled=True
    )


def local(
    ways, rows_ways, inputs, cotangent, segment, norm_gain, w_query, w_key, w_value, w_beta,
    conv_query, conv_key, conv_value, head_gain, w_out, ffn_gain, w_gate, w_up, w_down,
):
    micro, tokens, block = inputs.shape
    width = block * ways
    heads = w_beta.shape[1]
    hw = heads * 128
    per = tokens // SEQ
    here = lax.axis_index("col")
    spot = here.astype(jnp.int32)[None]

    share, taps_share = norm_gain.shape[0], conv_query.size
    packed = jnp.concatenate(
        [norm_gain, ffn_gain]
        + [taps.reshape(-1) for taps in (conv_query, conv_key, conv_value)]
        + [head_gain]
    )
    row = lax.axis_index("row")
    packed = lax.dynamic_update_slice(
        jnp.zeros((ways * rows_ways, packed.shape[0]), BF), packed[None], (here * rows_ways + row, 0)
    )
    packed = sum_over(packed, "col", ways, 2)
    first_share = after(inputs[0], packed)
    packed = sum_over(sum_over(packed, "col", 2, 1, ways), "row", rows_ways)
    gain_one = packed[:, :share].reshape(1, width).astype(F32)
    gain_two = packed[:, share : 2 * share].reshape(1, width).astype(F32)
    mine = lax.dynamic_slice_in_dim(packed, here * rows_ways, rows_ways, axis=0).astype(F32)
    taps = mine[:, 2 * share : 2 * share + 3 * taps_share]
    taps = taps.reshape(rows_ways, 3, share, 4).transpose(3, 1, 0, 2).reshape(4, 3 * hw)
    taps = jnp.pad(taps, ((0, 4), (0, 0)))
    gain_head = mine[:, 2 * share + 3 * taps_share :].reshape(1, 128)
    own_one = lax.dynamic_slice_in_dim(gain_one, here * block, block, axis=1)
    own_two = lax.dynamic_slice_in_dim(gain_two, here * block, block, axis=1)

    beta_wide = jnp.pad(w_beta, ((0, 0), (0, 128 - heads)))
    qkv_share = jnp.concatenate([w_query, w_key, w_value, beta_wide], axis=1)
    qkv = lax.all_gather(qkv_share, "row", axis=0, tiled=False)
    out_parts = lax.all_gather(w_out, "row", axis=0, tiled=False)
    gates = lax.all_gather(w_gate.T, "row", axis=0, tiled=False)
    ups = lax.all_gather(w_up.T, "row", axis=0, tiled=False)
    down = lax.all_gather(w_down, "row", axis=0, tiled=False)

    data = [token_marks(segment[m].reshape(per, SEQ), CHUNK) for m in range(micro)]
    x_base, cot_base, mine = [], [], first_share
    for m in range(micro):
        x_base.append(gather_cols(mine, ways, "split"))
        if m < micro - 1:
            mine = after(inputs[m + 1], arrays_of(x_base[m])[:3])
    for m in range(micro):
        mine = after(cotangent[m], arrays_of(x_base[m]))
        cot_base.append(gather_cols(mine, ways, "split"))
    weight = qkv.reshape(width, -1)
    pres, act_ones, inv_ones, mixed, saved = [], [], [], [], []
    resids, act_base = [], []

    def add_residual(m, own, arrived):
        resids.append(inputs[m].astype(F32) + total_of(own, arrived))
        act_base.append(gather_cols(resids[m].astype(BF), ways, "direct" if m else "split"))

    flying = None
    for m in range(micro):
        pieces = other_core(x_base[m], ways)
        if m:
            pieces = pieces_after(pieces, sums)
        pre, act, stat = project(pieces, gain_one, weight, spot, block)
        if m:
            pre, arrived = covered(pre, send_pairs(sums, ways))
            own, pairs = add_pairs(sums, arrived)
            flying = own, scatter_cols(pairs, ways)
            pre, cot_base[m] = covered(after(pre, arrays_of(pairs)), cot_base[m])
            if m == micro - 1:
                pre, gates, ups = lax.optimization_barrier((pre, gates, ups))
        elif micro > 1:
            pre, x_base[m + 1] = covered(pre, x_base[m + 1])
        pres.append(pre.reshape(per, SEQ, -1))
        act_ones.append(act)
        inv_ones.append(stat[:, 0:1])
        array, rest = mix_forward(pres[m], data[m], taps, gain_head, heads)
        if m == 0:
            array, cot_base[m] = covered(array, cot_base[m])
        mixed.append(array.reshape(tokens, hw))
        saved.append(rest)
        sums = spread(mixed[m], out_parts, spot, block, ways, False)
        if flying:
            sums, arrived = covered(sums, flying[1])
            add_residual(m - 1, flying[0], arrived)
            sums = after(sums, resids[m - 1])
        if m == micro - 1:
            sums, down = lax.optimization_barrier((sums, down))
    own, pairs = add_pairs(sums, send_pairs(sums, ways))
    flying = own, scatter_cols(pairs, ways)
    cots = [other_core(base, ways) for base in cot_base]

    ffn_saved, ffn_outs, inners, resid_grads, grad_base = [], [], [], [], []
    down_terms, gate_terms, up_terms, gain_two_grad = [], [], [], 0.0

    def finish_ffn(m, own, arrived):
        inverse = ffn_saved[m][5][:, 0:1]
        act_grad = total_of(own, arrived)
        unit = resids[m] * inverse
        resid_grads.append(
            cotangent[m].astype(F32) + inverse * (act_grad * own_two - unit * inners[m])
        )
        grad_base.append(gather_cols(resid_grads[m].astype(BF), ways))
        return jnp.sum(act_grad * unit, axis=0)

    for m in range(micro):
        pieces = other_core(act_base[m], ways)
        if m:
            pieces = pieces_after(pieces, up_terms, inners)
        else:
            pieces = pieces_after(pieces, arrays_of(pairs))
        kept, grads, outs = feed_forward(
            pieces, cots[m], gain_two, gates, ups, down, spot, block, ways
        )
        (kept, grads, outs), arrived = covered((kept, grads, outs), flying[1])
        if m < micro - 1:
            add_residual(m + 1, flying[0], arrived)
            kept, grads = after((kept, grads), resids[m + 1])
        else:
            gain_two_grad = gain_two_grad + finish_ffn(m - 1, flying[0], arrived)
            kept, grads = after((kept, grads), resid_grads[m - 1])
        ffn_saved.append(kept)
        inners.append(sum_over(kept[5][:, 1], "col", ways)[:, None] / width)
        term, arrived = covered(dot_tn(kept[2], kept[1]), send_pairs(grads, ways))
        down_terms.append(term)
        own, pairs = add_pairs(grads, arrived)
        flying = own, scatter_cols(pairs, ways)
        gate_term = dot_tn(kept[3], after(kept[0], arrays_of(pairs)))
        base = act_base[m + 1] if m < micro - 1 else grad_base[0]
        gate_term, arrived = covered(gate_term, send_pairs(outs, ways))
        gate_terms.append(gate_term)
        ffn_outs.append(add_pairs(outs, arrived))
        up_term = dot_tn(kept[4], after(kept[0], gate_term, arrays_of(ffn_outs[m][1])))
        up_term, base = covered(up_term, base)
        if m < micro - 1:
            act_base[m + 1] = base
        up_terms.append(up_term)
    pieces = other_core(base, ways)
    grad_down = scatter_row(sum(down_terms), 1)
    grad_gate = scatter_row(sum(gate_terms), 1)
    grad_up = scatter_row(sum(up_terms), 1)
    qkv_terms, out_terms, means, firsts, dconv, dgain = [], [], [], [], 0.0, 0.0
    behind, outputs = None, []
    for m in range(micro):
        whole, dao = collect(pieces, out_parts, spot, block, ways)
        own, sums = ffn_outs[m]
        out_flying = scatter_cols(pieces_after(sums, arrays_of(pieces)), ways)
        dpre, stat, dconv_part, dgain_part = mix_backward(
            pres[m], data[m], taps, gain_head, saved[m], dao.reshape(per, SEQ, hw), heads
        )
        dpre = dpre.reshape(tokens, -1)
        if m == micro - 1:
            dpre, grad_down, grad_gate = lax.optimization_barrier((dpre, grad_down, grad_gate))
        dconv, dgain = dconv + dconv_part, dgain + dgain_part
        if flying:
            dpre, arrived = covered(dpre, flying[1])
            gain_two_grad = gain_two_grad + finish_ffn(micro - 1, flying[0], arrived)
            dpre, flying = after(dpre, resid_grads[-1]), None
        dpre, arrived = covered(dpre, out_flying)
        outputs.append((resids[m] + total_of(own, arrived)).astype(BF))
        if behind:
            dpre, arrived = covered(dpre, behind[1])
            firsts.append(total_of(behind[0], arrived))
        if m < micro - 1:
            sums = spread(dpre, qkv, spot, block, ways, True)
            term, arrived = covered(
                dot_tn(act_ones[m], after(dpre, sums)), send_pairs(sums, ways)
            )
            own, pairs = add_pairs(sums, arrived)
            behind = own, scatter_cols(pairs, ways)
            out_term = dot_tn(mixed[m], after(whole, arrays_of(pairs)))
            out_term, grad_base[m + 1] = covered(out_term, grad_base[m + 1])
            pieces = pieces_after(other_core(grad_base[m + 1], ways), out_term)
        else:
            term = dot_tn(act_ones[m], dpre)
            sums = spread(after(dpre, term), qkv, spot, block, ways, True)
            out_term = dot_tn(mixed[m], after(whole, sums))
            out_term, arrived = covered(out_term, send_pairs(sums, ways))
            own, pairs = add_pairs(sums, arrived)
            firsts.append(total_of(own, scatter_cols(pairs, ways, "direct")))
        qkv_terms.append(term)
        out_terms.append(out_term)
        means.append(sum_over(stat.reshape(tokens, 128)[:, 0], "col", ways)[:, None] / width)
    grad_qkv = scatter_row(sum(qkv_terms), 0)
    grad_out = scatter_row(sum(out_terms), 1)
    input_grads, gain_one_grad = [], 0.0
    for m in range(micro):
        unit = inputs[m].astype(F32) * inv_ones[m]
        gain_one_grad = gain_one_grad + jnp.sum(firsts[m] * unit, axis=0)
        input_grads.append(
            resid_grads[m] + inv_ones[m] * (firsts[m] * own_one - unit * means[m])
        )

    grad_qkv, grad_out, grad_gate, grad_up, grad_down = (
        grad.astype(F32) for grad in (grad_qkv, grad_out, grad_gate, grad_up, grad_down)
    )
    head_sum = sum_over(jnp.sum(dgain, axis=0), "col", ways)
    conv_sum = dconv.reshape(4, 8, 3, hw).sum(axis=1).transpose(1, 2, 0)
    early = sum_over(
        jnp.concatenate([conv_sum.reshape(-1), head_sum, gain_two_grad]), "row", rows_ways
    )
    late = sum_over(gain_one_grad, "row", rows_ways)
    conv_grads = lax.dynamic_slice_in_dim(
        early[: 12 * hw].reshape(3, hw, 4), row * share, share, axis=1
    )
    grad_head = lax.dynamic_slice_in_dim(
        early[12 * hw : 12 * hw + 128], row * head_gain.shape[0], head_gain.shape[0]
    )
    grad_two = lax.dynamic_slice_in_dim(early[12 * hw + 128 :], row * share, share)
    grad_one = lax.dynamic_slice_in_dim(late, row * share, share)
    return (
        jnp.stack(outputs),
        jnp.stack(input_grads),
        grad_one,
        grad_qkv[:, :hw],
        grad_qkv[:, hw : 2 * hw],
        grad_qkv[:, 2 * hw : 3 * hw],
        grad_qkv[:, 3 * hw : 3 * hw + heads],
        conv_grads[0],
        conv_grads[1],
        conv_grads[2],
        grad_head,
        grad_out,
        grad_two,
        grad_gate.T,
        grad_up.T,
        grad_down,
    )


def solution(mesh):
    both = P(("col", "row"))
    taps = P(("col", "row"), None)
    rows_cols, cols_rows = P("row", "col"), P("col", "row")
    tokens = P(None, "row", "col")
    in_specs = (
        tokens, tokens, P(None, "row"), both, rows_cols, rows_cols, rows_cols, rows_cols,
        taps, taps, taps, P("row"), cols_rows, both, rows_cols, rows_cols, cols_rows,
    )
    out_specs = (
        tokens, tokens, both, rows_cols, rows_cols, rows_cols, rows_cols,
        taps, taps, taps, P("row"), cols_rows, both, rows_cols, rows_cols, cols_rows,
    )
    body = partial(local, mesh.shape["col"], mesh.shape["row"])
    return jax.shard_map(body, mesh=mesh, in_specs=in_specs, out_specs=out_specs, check_vma=False)
```

```python
from functools import partial

import jax
import jax.numpy as jnp
from jax import lax
from jax.experimental import pallas as pl
from jax.experimental.pallas import tpu as pltpu
from jax.sharding import PartitionSpec as P

SEQ = 2048
CHUNK = 128
FWD_SUB = 4
BWD_SUB = 2
TILE = 512
HALO = 8
EPSILON = 1e-06
HEAD_FLOOR = 0.002
BF = jnp.bfloat16
F32 = jnp.float32
FFN_TILE = 256
PER_MICRO = 4.0e8


def dot_nn(a, b):
    return lax.dot_general(a, b, (((1,), (0,)), ((), ())), preferred_element_type=F32)


def dot_nt(a, b):
    return lax.dot_general(a, b, (((1,), (1,)), ((), ())), preferred_element_type=F32)


def dot_tn(a, b):
    return lax.dot_general(a, b, (((0,), (0,)), ((), ())), preferred_element_type=F32)


def token_marks(labels, chunk):
    seqs, length = labels.shape
    padded_back = jnp.pad(labels, ((0, 0), (4, 0)), constant_values=-1)
    padded_fore = jnp.pad(labels, ((0, 0), (0, 4)), constant_values=-2)
    marks = [labels]
    for lag in (1, 2, 3):
        marks.append(padded_back[:, 4 - lag : 4 - lag + length] == labels)
    for lag in (1, 2, 3):
        marks.append(padded_fore[:, lag : lag + length] == labels)
    grid = labels.reshape(seqs, length // chunk, chunk)
    prior = jnp.pad(grid[:, :-1, -1], ((0, 0), (1, 0)), constant_values=-1)
    marks.append((grid == prior[:, :, None]).reshape(seqs, length))
    marks.append((grid == grid[:, :, -1:]).reshape(seqs, length))
    marks.append(
        jnp.broadcast_to((grid[:, :, -1] == prior)[:, :, None], grid.shape).reshape(seqs, length)
    )
    marks += [jnp.zeros_like(labels)] * (16 - len(marks))
    marks = [mark.astype(F32).reshape(seqs, length // chunk, 1, chunk) for mark in marks]
    return jnp.concatenate(marks, axis=2)


LABEL, BACK, FORE, CARRIED, LAST, KEEP = 0, 0, 3, 7, 8, 9


def sigmoid(x):
    return 1.0 / (1.0 + jnp.exp(-x))


def level_marks(size):
    row = lax.broadcasted_iota(jnp.int32, (size, size), 0)
    col = lax.broadcasted_iota(jnp.int32, (size, size), 1)
    return row == col, row ^ col


def unit_lower_inverses(systems):
    size = systems[0].shape[0]
    diagonal, differ = level_marks(size)
    inverses = [
        (jnp.where(diagonal, 1.0, 0.0) - jnp.where(differ == 1, system, 0.0)).astype(BF)
        for system in systems
    ]
    block = 2
    while block < size:
        level = (differ >= block) & (differ < 2 * block)
        offs = [jnp.where(level, system, 0.0).astype(BF) for system in systems]
        lefts = [dot_nn(inverse, off).astype(BF) for inverse, off in zip(inverses, offs)]
        inverses = [
            inverse - dot_nn(left, inverse).astype(BF) for inverse, left in zip(inverses, lefts)
        ]
        block *= 2
    return inverses


def conv_rows(ext, taps, marks, lane, first, chunk):
    here = ext[pl.ds(HALO + first, chunk), lane]
    shifted = [here]
    total = here * taps[0:1, lane]
    for lag in (1, 2, 3):
        moved = ext[pl.ds(HALO + first - lag, chunk), lane] * marks[:, BACK + lag : BACK + lag + 1]
        shifted.append(moved)
        total = total + moved * taps[lag : lag + 1, lane]
    return total, shifted


def chunk_marks(marks_ref, seq, part, chunk):
    by_row = marks_ref[seq, part]
    marks = jnp.transpose(by_row)
    row = lax.broadcasted_iota(jnp.int32, (chunk, chunk), 0)
    col = lax.broadcasted_iota(jnp.int32, (chunk, chunk), 1)
    same = marks[:, LABEL : LABEL + 1] == by_row[LABEL : LABEL + 1, :]
    return (
        marks,
        same & (row > col),
        same & (row >= col),
        marks[:, CARRIED : CARRIED + 1],
        marks[:, LAST : LAST + 1],
        marks[0:1, KEEP : KEEP + 1],
    )


def mix_fwd_kernel(
    heads, chunk, sub, marks_ref, taps_ref, gain_ref, pre_ref,
    ao_ref, o_ref, u_ref, w_ref, state_ref, inv_ref, ext, memory,
):
    seqs = pre_ref.shape[0]
    wide = 3 * heads * 128
    size = sub * chunk

    @pl.when(pl.program_id(0) == 0)
    def _():
        ext[:, 0:HALO, :] = jnp.zeros((seqs, HALO, wide), F32)
        memory[...] = jnp.zeros_like(memory)

    ext[:, HALO : HALO + size, :] = pre_ref[:, :, 0:wide]
    kept = {
        (seq, part): chunk_marks(marks_ref, seq, part, chunk)
        for seq in range(seqs)
        for part in range(sub)
    }
    chains = [(seq, head) for seq in range(seqs) for head in range(heads)]
    units = [(seq, head, part) for part in range(sub) for seq, head in chains]
    boths, values, betas, attns, keys_list, systems = {}, {}, {}, {}, {}, {}
    for unit in units:
        seq, head, part = unit
        marks = kept[seq, part][0]
        acts = []
        for kind in range(3):
            lane = pl.ds((kind * heads + head) * 128, 128)
            cv, _ = conv_rows(ext.at[seq], taps_ref, marks, lane, part * chunk, chunk)
            acts.append(cv * sigmoid(cv))
        q1, k1, values[unit] = acts
        qn = q1 * (lax.rsqrt(jnp.sum(q1 * q1, axis=1, keepdims=True) + EPSILON) * 128 ** (-0.5))
        kn = k1 * lax.rsqrt(jnp.sum(k1 * k1, axis=1, keepdims=True) + EPSILON)
        betas[unit] = sigmoid(
            pre_ref[seq, part * chunk : (part + 1) * chunk, wide + head : wide + head + 1]
        )
        boths[unit] = jnp.concatenate([qn.astype(BF), kn.astype(BF)], axis=0)
    for unit in units:
        _, strict, within, _, _, _ = kept[unit[0], unit[2]]
        scores = dot_nt(boths[unit], boths[unit][chunk:])
        attns[unit] = jnp.where(within, scores[:chunk], 0.0).astype(BF)
        keys = jnp.where(strict, scores[chunk:], 0.0)
        keys_list[unit] = keys.astype(BF)
        systems[unit] = keys * betas[unit]
    inverses = dict(zip(units, unit_lower_inverses([systems[unit] for unit in units])))
    for part in range(sub):
        here = [(seq, head, part) for seq, head in chains]
        states = [memory[index] for index in range(len(here))]
        lows = [state.astype(BF) for state in states]
        seens = [dot_nn(boths[unit], low) for unit, low in zip(here, lows)]
        rights = [
            values[unit] - kept[unit[0], part][3] * seen[chunk:]
            for unit, seen in zip(here, seens)
        ]
        updates = [
            dot_nn(inverses[unit], (betas[unit] * right).astype(BF))
            for unit, right in zip(here, rights)
        ]
        for index, unit in enumerate(here):
            last, keep = kept[unit[0], part][4:]
            memory[index] = keep * states[index] + dot_tn(
                boths[unit][chunk:], (last * updates[index]).astype(BF)
            )
        for index, unit in enumerate(here):
            seq, head, _ = unit
            carried = kept[seq, part][3]
            rows = slice(part * chunk, (part + 1) * chunk)
            ub = updates[index].astype(BF)
            mixed = dot_nn(jnp.concatenate([attns[unit], keys_list[unit]], axis=0), ub)
            out = carried * seens[index][:chunk] + mixed[:chunk]
            wrong = rights[index] - mixed[chunk:]
            lane = pl.ds(head * 128, 128)
            scale = lax.rsqrt(jnp.maximum(jnp.mean(out * out, axis=1, keepdims=True), HEAD_FLOOR))
            ao_ref[seq, rows, lane] = (out * scale * gain_ref[...]).astype(BF)
            o_ref[seq, rows, lane] = out
            u_ref[seq, rows, lane] = ub
            w_ref[seq, rows, lane] = wrong.astype(BF)
            inv_ref[part, index] = inverses[unit]
            state_ref[part, index] = lows[index]
    ext[:, 0:HALO, :] = ext[:, size : size + HALO, :]


def mix_bwd_kernel(
    heads, chunk, sub, marks_ref, taps_ref, gain_ref,
    o_ref, u_ref, w_ref, state_ref, inv_ref, pre_ref, halo_ref, dao_ref,
    dpre_ref, stat_ref, dconv_ref, dgain_ref, ext, dext, memory,
):
    seqs = pre_ref.shape[0]
    wide = 3 * heads * 128
    size = sub * chunk

    @pl.when(pl.program_id(0) == 0)
    def _():
        dext[:, size : size + HALO, :] = jnp.zeros((seqs, HALO, wide), F32)
        memory[...] = jnp.zeros_like(memory)
        dconv_ref[...] = jnp.zeros_like(dconv_ref)
        dgain_ref[...] = jnp.zeros_like(dgain_ref)

    ext[:, 0:HALO, :] = halo_ref[:, :, 0:wide]
    ext[:, HALO : HALO + size, :] = pre_ref[:, :, 0:wide]
    gain = gain_ref[...]

    def fold(rows):
        return jnp.sum(rows.reshape(chunk // 8, 8, 128), axis=0)

    kept = {
        (seq, part): chunk_marks(marks_ref, seq, part, chunk)
        for seq in range(seqs)
        for part in range(sub)
    }
    chains = [(seq, head) for seq in range(seqs) for head in range(heads)]
    units = [(seq, head, part) for part in reversed(range(sub)) for seq, head in chains]

    def rows_of(unit):
        return slice(unit[2] * chunk, (unit[2] + 1) * chunk)

    def lane_of(unit, kind=0):
        return pl.ds((kind * heads + unit[1]) * 128, 128)

    acts, scales, norms, betas, boths, dobs, cdos = {}, {}, {}, {}, {}, {}, {}
    for unit in units:
        seq, head, part = unit
        marks, _, _, carried, _, _ = kept[seq, part]
        for kind in range(3):
            cv, _ = conv_rows(
                ext.at[seq], taps_ref, marks, lane_of(unit, kind), part * chunk, chunk
            )
            sg = sigmoid(cv)
            acts[unit, kind] = cv * sg
            scales[unit, kind] = sg * (1.0 + cv * (1.0 - sg))
        q1, k1 = acts[unit, 0], acts[unit, 1]
        rq = lax.rsqrt(jnp.sum(q1 * q1, axis=1, keepdims=True) + EPSILON)
        rk = lax.rsqrt(jnp.sum(k1 * k1, axis=1, keepdims=True) + EPSILON)
        norms[unit] = rq, rk
        boths[unit] = jnp.concatenate(
            [(q1 * (rq * 128 ** (-0.5))).astype(BF), (k1 * rk).astype(BF)], axis=0
        )
        betas[unit] = sigmoid(pre_ref[seq, rows_of(unit), wide + head : wide + head + 1])
        out = o_ref[seq, rows_of(unit), lane_of(unit)]
        square = jnp.mean(out * out, axis=1, keepdims=True)
        scale = lax.rsqrt(jnp.maximum(square, HEAD_FLOOR))
        ro = out * scale
        dao = dao_ref[seq, rows_of(unit), lane_of(unit)]
        dgain_ref[...] += fold(dao * ro)
        eo = dao * gain
        inner = jnp.mean(eo * ro, axis=1, keepdims=True)
        inner = jnp.where(square > HEAD_FLOOR, inner, 0.0)
        do = scale * (eo - ro * inner)
        dobs[unit] = do.astype(BF)
        cdos[unit] = (carried * do).astype(BF)
    firsts, grows, crosses = {}, {}, {}
    for unit in units:
        _, _, within, _, _, _ = kept[unit[0], unit[2]]
        both = boths[unit]
        attn = jnp.where(within, dot_nt(both[:chunk], both[chunk:]), 0.0).astype(BF)
        firsts[unit] = dot_tn(attn, dobs[unit])
        grows[unit] = dot_tn(both[:chunk], cdos[unit])
    drs, seconds, dbetas = {}, {}, {}
    for part in reversed(range(sub)):
        here = [(seq, head, part) for seq, head in chains]
        olds = [memory[index] for index in range(len(here))]
        lows = [old.astype(BF) for old in olds]
        fromstate = [dot_nn(boths[unit][chunk:], low) for unit, low in zip(here, lows)]
        dus = [
            (firsts[unit] + kept[unit[0], part][4] * term).astype(BF)
            for unit, term in zip(here, fromstate)
        ]
        drhs = [dot_tn(inv_ref[part, index], du) for index, du in enumerate(dus)]
        for index, unit in enumerate(here):
            drs[unit] = betas[unit] * drhs[index]
            carried, _, keep = kept[unit[0], part][3:]
            memory[index] = (
                keep * olds[index]
                + grows[unit]
                - dot_tn(boths[unit][chunk:], (carried * drs[unit]).astype(BF))
            )
        for index, unit in enumerate(here):
            wrong = w_ref[unit[0], rows_of(unit), lane_of(unit)].astype(F32)
            dbetas[unit] = jnp.sum(drhs[index] * wrong, axis=1, keepdims=True)
            seconds[unit] = dot_nt(u_ref[unit[0], rows_of(unit), lane_of(unit)], lows[index])
    shares = {}
    for unit in units:
        seq, head, part = unit
        marks, strict, within, carried, last, _ = kept[seq, part]
        both, kb = boths[unit], boths[unit][chunk:]
        index = seq * heads + head
        stack = jnp.concatenate([dobs[unit], drs[unit].astype(BF)], axis=0)
        right = jnp.concatenate(
            [u_ref[seq, rows_of(unit), lane_of(unit)], state_ref[part, index]], axis=0
        )
        cross = dot_nt(stack, right)
        dattn = jnp.where(within, cross[:chunk, :chunk], 0.0).astype(BF)
        dkeys = jnp.where(strict, -cross[chunk:, :chunk], 0.0).astype(BF)
        dboth = jnp.concatenate([dattn, dkeys], axis=0)
        by_row = dot_nn(dboth, kb)
        dqn = carried * cross[:chunk, chunk:] + by_row[:chunk]
        dkn = (
            dot_tn(dboth, both)
            + last * seconds[unit]
            + by_row[chunk:]
            - carried * cross[chunk:, chunk:]
        )
        (rq, rk), q1, k1 = norms[unit], acts[unit, 0], acts[unit, 1]
        dq1 = 128 ** (-0.5) * rq * (
            dqn - (rq * rq) * q1 * jnp.sum(q1 * dqn, axis=1, keepdims=True)
        )
        dk1 = rk * (dkn - (rk * rk) * k1 * jnp.sum(k1 * dkn, axis=1, keepdims=True))
        for kind, dact in enumerate((dq1, dk1, drs[unit])):
            dext[seq, rows_of(unit), lane_of(unit, kind)] = dact * scales[unit, kind]
    for unit in units:
        seq, head, part = unit
        marks = kept[seq, part][0]
        share = shares.get((seq, part), 0.0)
        for kind in range(3):
            lane = lane_of(unit, kind)
            _, shifts = conv_rows(ext.at[seq], taps_ref, marks, lane, part * chunk, chunk)
            dc = dext[seq, rows_of(unit), lane]
            back = dc * taps_ref[0:1, lane]
            dconv_ref[0:8, lane] += fold(dc * shifts[0])
            for lag in (1, 2, 3):
                dconv_ref[8 * lag : 8 * lag + 8, lane] += fold(dc * shifts[lag])
                back = back + (
                    dext[seq, pl.ds(part * chunk + lag, chunk), lane]
                    * marks[:, FORE + lag : FORE + lag + 1]
                    * taps_ref[lag : lag + 1, lane]
                )
            dpre_ref[seq, rows_of(unit), lane] = back.astype(BF)
            share = share + back * shifts[0]
        shares[seq, part] = share
    column = lax.broadcasted_iota(jnp.int32, (chunk, 128), 1)
    for seq, part in kept:
        rows = slice(part * chunk, (part + 1) * chunk)
        total = jnp.zeros((chunk, 128), F32)
        for head in range(heads):
            unit = seq, head, part
            grad = dbetas[unit] * betas[unit] * (1.0 - betas[unit])
            total = jnp.where(column == head, grad, total)
        dpre_ref[seq, rows, pl.ds(wide, 128)] = total.astype(BF)
        share = shares[seq, part] + total * pre_ref[seq, rows, pl.ds(wide, 128)]
        stat_ref[seq, rows] = jnp.broadcast_to(
            jnp.sum(share, axis=1, keepdims=True), (chunk, 128)
        )
    dext[:, size : size + HALO, :] = dext[:, 0:HALO, :]


def params():
    return pltpu.CompilerParams(dimension_semantics=("arbitrary",), vmem_limit_bytes=60 * 2**20)


def fixed(array):
    zeros = (0,) * array.ndim
    return pl.BlockSpec(array.shape, lambda n: zeros, pipeline_mode=pl.Buffered(1))


def cost(micros):
    return pl.CostEstimate(flops=int(micros * PER_MICRO), bytes_accessed=0, transcendentals=0)


def shape(dims, dtype):
    return jax.ShapeDtypeStruct(dims, dtype)


def mix_forward(pre, marks, taps, gain, heads, chunk=CHUNK, sub=FWD_SUB):
    seqs, length, cols = pre.shape
    chains, parts = seqs * heads, length // chunk
    steps = parts // sub
    wide, hw = 3 * heads * 128, heads * 128

    def tok(width):
        return pl.BlockSpec((seqs, sub * chunk, width), lambda n: (0, n, 0))

    out_shape = [
        shape((seqs, length, hw), BF),
        shape((seqs, length, hw), F32),
        shape((seqs, length, hw), BF),
        shape((seqs, length, hw), BF),
        shape((parts, chains, 128, 128), BF),
        shape((parts, chains, chunk, chunk), BF),
    ]
    mixed, *saved = pl.pallas_call(
        partial(mix_fwd_kernel, heads, chunk, sub),
        grid=(steps,),
        in_specs=[
            pl.BlockSpec((seqs, sub, 16, chunk), lambda n: (0, n, 0, 0)),
            fixed(taps), fixed(gain), tok(cols),
        ],
        out_specs=[tok(hw)] * 4 + [
            pl.BlockSpec((sub, chains, 128, 128), lambda n: (n, 0, 0, 0)),
            pl.BlockSpec((sub, chains, chunk, chunk), lambda n: (n, 0, 0, 0)),
        ],
        out_shape=out_shape,
        scratch_shapes=[
            pltpu.VMEM((seqs, HALO + sub * chunk, wide), F32),
            pltpu.VMEM((chains, 128, 128), F32),
        ],
        compiler_params=params(),
        cost_estimate=cost(24),
        name="mix_forward",
    )(marks, taps, gain, pre)
    return mixed, saved


def mix_backward(pre, marks, taps, gain, saved, dao, heads, chunk=CHUNK, sub=BWD_SUB):
    seqs, length, cols = pre.shape
    chains, parts = seqs * heads, length // chunk
    steps = parts // sub
    wide, hw = 3 * heads * 128, heads * 128
    end, groups = steps - 1, sub * chunk // HALO

    def tok(width):
        return pl.BlockSpec((seqs, sub * chunk, width), lambda n: (0, end - n, 0))

    halo = pl.BlockSpec(
        (seqs, HALO, cols), lambda n: (0, jnp.maximum((end - n) * groups - 1, 0), 0)
    )
    out_shape = [
        shape((seqs, length, cols), BF), shape((seqs, length, 128), F32),
        shape((32, wide), F32), shape((8, 128), F32),
    ]
    return pl.pallas_call(
        partial(mix_bwd_kernel, heads, chunk, sub),
        grid=(steps,),
        in_specs=[
            pl.BlockSpec((seqs, sub, 16, chunk), lambda n: (0, end - n, 0, 0)),
            fixed(taps), fixed(gain),
        ] + [tok(hw)] * 3 + [
            pl.BlockSpec((sub, chains, 128, 128), lambda n: (end - n, 0, 0, 0)),
            pl.BlockSpec((sub, chains, chunk, chunk), lambda n: (end - n, 0, 0, 0)),
            tok(cols), halo, tok(hw),
        ],
        out_specs=[
            tok(cols), tok(128),
            pl.BlockSpec((32, wide), lambda n: (0, 0)),
            pl.BlockSpec((8, 128), lambda n: (0, 0)),
        ],
        out_shape=out_shape,
        scratch_shapes=[
            pltpu.VMEM((seqs, HALO + sub * chunk, wide), F32),
            pltpu.VMEM((seqs, HALO + sub * chunk, wide), F32),
            pltpu.VMEM((chains, 128, 128), F32),
        ],
        compiler_params=params(),
        cost_estimate=cost(34),
        name="mix_backward",
    )(marks, taps, gain, *saved, pre, pre, dao)


def swap(values, bit, ways):
    return lax.ppermute(values, "col", [(i, i ^ bit) for i in range(ways)])


def gather_near(values, ways):
    base = [(0, 0, values)]
    if ways == 8:
        return base + [(far, 0, swap(values, far, ways)) for far in (2, 4)]
    bit = 2
    while bit < ways:
        base += [(far ^ bit, lane, swap(array, bit, ways)) for far, lane, array in base]
        bit *= 2
    return base


def gather_far(base, ways, *others):
    if ways != 8:
        return base
    along, across = base[1][2], base[2][2]
    half = along.shape[-1] // 2
    first, second = across[..., :half], along[..., half:]
    if others:
        first, second = after((first, second), others)
    return base + [(6, 0, swap(first, 2, ways)), (6, half, swap(second, 4, ways))]


def gather_cols(values, ways, way="direct"):
    base = gather_near(values, ways)
    if ways != 8 or way == "split":
        return gather_far(base, ways)
    return base + [(6, 0, swap(values, 6, ways))]


def other_core(base, ways):
    return base + [(far ^ 1, lane, swap(array, 1, ways)) for far, lane, array in base]


def after(values, *others):
    return lax.optimization_barrier((values, others))[0]


def arrays_of(pieces):
    return [array for _, _, array in pieces]


def pieces_after(pieces, *others):
    arrays = after(arrays_of(pieces), *others)
    return [(far, lane, array) for (far, lane, _), array in zip(pieces, arrays)]


def covered(results, pieces):
    results, arrays = lax.optimization_barrier((results, arrays_of(pieces)))
    return results, [(far, lane, array) for (far, lane, _), array in zip(pieces, arrays)]


def add_low(*terms):
    return sum(term.astype(F32) for term in terms).astype(BF)


def send_pairs(pieces, ways):
    return [(far, 0, swap(pieces[far | 1], 1, ways)) for far in range(0, ways, 2)]


def add_pairs(pieces, arrived):
    sums = [(far, 0, add_low(pieces[far], array)) for far, _, array in arrived if far]
    return (pieces[0], arrived[0][2]), sums


def scatter_cols(sums, ways, way="direct"):
    held = {far: array for far, _, array in sums}
    if ways == 8 and way == "direct":
        return [(far, 0, swap(held[far], far, ways)) for far in (2, 4, 6)]
    if ways == 8:
        half = held[2].shape[-1] // 2
        left = swap(held[6][..., :half], 2, ways)
        right = swap(held[6][..., half:], 4, ways)
        four = jnp.concatenate(
            [add_low(left, held[4][..., :half]), held[4][..., half:]], axis=-1
        )
        two = jnp.concatenate(
            [held[2][..., :half], add_low(right, held[2][..., half:])], axis=-1
        )
        return [(2, 0, swap(two, 2, ways)), (4, 0, swap(four, 4, ways))]
    terms = {far: (array,) for far, array in held.items()}
    terms[0] = ()
    bit = 2
    while bit < ways:
        terms = {
            far: terms[far] + (swap(add_low(*terms[far | bit]), bit, ways),)
            for far in terms
            if not far & bit
        }
        bit *= 2
    return [(0, 0, array) for array in terms[0]]


def total_of(own, arrived):
    return sum(array.astype(F32) for array in (*own, *arrays_of(arrived)))


def sum_over(values, axis, ways, bit=1, size=None):
    size = ways if size is None else size
    while bit < ways:
        values = values + lax.ppermute(values, axis, [(i, i ^ bit) for i in range(size)])
        bit *= 2
    return values


def sum_cols(values, ways):
    values = values + swap(values, 1, ways)
    return values + sum(swap(values, far, ways) for far in range(2, ways, 2))


def whole_blocks(layout, pieces):
    blocks = {}
    for (far, _), piece in zip(layout, pieces):
        blocks.setdefault(far, []).append(piece[...])
    return {
        far: parts[0] if len(parts) == 1 else jnp.concatenate(parts, axis=1)
        for far, parts in blocks.items()
    }


def lanes_of(spot_ref, far, block):
    return pl.ds(pl.multiple_of((spot_ref[0] ^ far) * block, block), block)


def part_of(spot_ref, far, block, step):
    index, each = spot_ref[0] ^ far, step // block
    return index // each, pl.ds(pl.multiple_of((index % each) * block, block), block)


def normed(blocks, spot_ref, gain_ref, act_ref, block):
    width = act_ref.shape[1]
    total = 0.0
    for rows in blocks.values():
        rows = rows.astype(F32)
        total = total + jnp.sum(rows * rows, axis=1, keepdims=True)
    inverse = lax.rsqrt(total / width + EPSILON)
    acts = {}
    for far, rows in blocks.items():
        lanes = lanes_of(spot_ref, far, block)
        acts[far] = (rows.astype(F32) * inverse * gain_ref[0:1, lanes]).astype(BF)
        act_ref[:, lanes] = acts[far]
    return acts, inverse


def project_kernel(layout, block, spot_ref, gain_ref, weight_ref, *refs):
    pieces, (pre_ref, act_ref, stat_ref) = refs[: len(layout)], refs[len(layout) :]
    blocks = whole_blocks(layout, pieces)
    acts, inverse = normed(blocks, spot_ref, gain_ref, act_ref, block)
    stat_ref[...] = jnp.broadcast_to(inverse, stat_ref.shape)
    total = 0.0
    for far, act in acts.items():
        total = total + dot_nn(act, weight_ref[lanes_of(spot_ref, far, block), :])
    pre_ref[...] = total


def spread_kernel(transposed, block, spot_ref, weight_ref, rows_ref, *outs):
    rows = rows_ref[...]
    step = weight_ref.shape[1 if transposed else 2]
    for far, out in enumerate(outs):
        part, lanes = part_of(spot_ref, far, block, step)
        if transposed:
            out[...] = dot_nt(rows, weight_ref[part, lanes, :]).astype(BF)
        else:
            out[...] = dot_nn(rows, weight_ref[part, :, lanes]).astype(BF)


def collect_kernel(layout, block, spot_ref, weight_ref, *refs):
    pieces, (whole_ref, out_ref) = refs[: len(layout)], refs[len(layout) :]
    for far, rows in whole_blocks(layout, pieces).items():
        whole_ref[:, lanes_of(spot_ref, far, block)] = rows
    step = weight_ref.shape[2]
    total = 0.0
    for part in range(weight_ref.shape[0]):
        total = total + dot_nt(
            whole_ref[:, part * step : (part + 1) * step], weight_ref[part]
        )
    out_ref[...] = total


def ffn_kernel(layout, cot_layout, block, ways, spot_ref, gain_ref, gates_ref, ups_ref, down_ref, *refs):
    count, total = len(layout), len(layout) + len(cot_layout)
    acts, cots, refs = refs[:count], refs[count:total], refs[total:]
    act_ref, cot_ref, hid_ref, dgate_ref, dup_ref, stat_ref = refs[:6]
    grads, outs = refs[6 : 6 + ways], refs[6 + ways : -4]
    whole, gates, ups, downs = refs[-4:]

    @pl.when(pl.program_id(0) == 0)
    def _():
        step = down_ref.shape[2]
        for part in range(down_ref.shape[0]):
            lanes = slice(part * step, (part + 1) * step)
            gates[:, lanes] = gates_ref[part]
            ups[:, lanes] = ups_ref[part]
            downs[:, lanes] = down_ref[part]

    for far, rows in whole_blocks(cot_layout, cots).items():
        cot_ref[:, lanes_of(spot_ref, far, block)] = rows
    _, inverse = normed(whole_blocks(layout, acts), spot_ref, gain_ref, act_ref, block)
    dhid = dot_nt(cot_ref[...], downs[...])
    gate = dot_nt(act_ref[...], gates[...])
    up = dot_nt(act_ref[...], ups[...])
    sig = sigmoid(gate)
    swish = gate * sig
    hid = (swish * up).astype(BF)
    dgate = (dhid * up * sig * (1.0 + gate * (1.0 - sig))).astype(BF)
    dup = (dhid * swish).astype(BF)
    hid_ref[...] = hid
    dgate_ref[...] = dgate
    dup_ref[...] = dup
    inner = jnp.sum(dgate.astype(F32) * gate + dup.astype(F32) * up, axis=1, keepdims=True)
    lane = lax.broadcasted_iota(jnp.int32, stat_ref.shape, 1)
    stat_ref[...] = jnp.where(lane == 0, inverse, inner)
    whole[...] = (dot_nn(dgate, gates[...]) + dot_nn(dup, ups[...])).astype(BF)
    for far, grad in enumerate(grads):
        grad[...] = whole[:, lanes_of(spot_ref, far, block)]
    if len(outs) == 1:
        outs[0][...] = dot_nn(hid, downs[...]).astype(BF)
    else:
        whole[...] = dot_nn(hid, downs[...]).astype(BF)
        for far, out in enumerate(outs):
            out[...] = whole[:, lanes_of(spot_ref, far, block)]


SPOT = pl.BlockSpec(memory_space=pltpu.SMEM)


def rows_spec(width, tile):
    return pl.BlockSpec((tile, width), lambda n: (n, 0))


def tiled(kernel, name, fixed_args, row_args, out_shape, tile, micros, spot, scratch=()):
    rows = row_args[0].shape[0]
    return pl.pallas_call(
        kernel,
        grid=(rows // tile,),
        in_specs=[SPOT]
        + [fixed(a) for a in fixed_args]
        + [rows_spec(a.shape[1], tile) for a in row_args],
        out_specs=[rows_spec(a.shape[1], tile) for a in out_shape],
        out_shape=out_shape,
        scratch_shapes=list(scratch),
        compiler_params=params(),
        cost_estimate=cost(micros),
        name=name,
    )(spot, *fixed_args, *row_args)


def layout_of(pieces):
    return tuple((far, lane) for far, lane, _ in pieces), [array for _, _, array in pieces]


def project(pieces, gain, weight, spot, block):
    layout, arrays = layout_of(pieces)
    rows, (width, cols) = arrays[0].shape[0], weight.shape
    out = [shape((rows, cols), F32), shape((rows, width), BF), shape((rows, 128), F32)]
    return tiled(
        partial(project_kernel, layout, block), "project", [gain, weight], arrays, out,
        TILE, 19, spot,
    )


def spread(rows_in, weight, spot, block, ways, transposed):
    rows = rows_in.shape[0]
    return tiled(
        partial(spread_kernel, transposed, block), "spread", [weight], [rows_in],
        [shape((rows, block), BF)] * ways, TILE, 14 if transposed else 7, spot,
    )


def collect(pieces, weight, spot, block, ways):
    layout, arrays = layout_of(pieces)
    rows = arrays[0].shape[0]
    out = [shape((rows, block * ways), BF), shape((rows, weight.shape[1]), F32)]
    return tiled(
        partial(collect_kernel, layout, block), "collect", [weight], arrays, out,
        TILE, 9, spot,
    )


def feed_forward(acts, cots, gain, gates, ups, down, spot, block, ways, split):
    layout, act_arrays = layout_of(acts)
    cot_layout, cot_arrays = layout_of(cots)
    rows, width, hidden = act_arrays[0].shape[0], block * ways, down.shape[1]
    out = (
        [shape((rows, width), BF)] * 2
        + [shape((rows, hidden), BF)] * 3
        + [shape((rows, 128), F32)]
        + [shape((rows, block), BF)] * ways
        + ([shape((rows, block), BF)] * ways if split else [shape((rows, width), BF)])
    )
    results = tiled(
        partial(ffn_kernel, layout, cot_layout, block, ways), "feed_forward", [gain, gates, ups, down],
        act_arrays + cot_arrays, out, FFN_TILE, 54, spot,
        [pltpu.VMEM((FFN_TILE, width), BF)] + [pltpu.VMEM((hidden, width), BF)] * 3,
    )
    return results[:6], results[6 : 6 + ways], results[6 + ways :]


def outer(lefts, rights):
    total = None
    for left, right in zip(lefts, rights):
        term = dot_tn(left, right)
        total = term if total is None else total + term
    return total


def grow(total, left, right, last):
    term = dot_tn(left, right)
    term = term if total is None else total + term
    return term.astype(BF) if last else term


def scatter_row(values, dim):
    return lax.psum_scatter(
        values.astype(BF), "row", scatter_dimension=dim, tiled=True
    )


def local(
    ways, rows_ways, inputs, cotangent, segment, norm_gain, w_query, w_key, w_value, w_beta,
    conv_query, conv_key, conv_value, head_gain, w_out, ffn_gain, w_gate, w_up, w_down,
):
    micro, tokens, block = inputs.shape
    width = block * ways
    heads = w_beta.shape[1]
    hw = heads * 128
    per = tokens // SEQ
    here = lax.axis_index("col")
    spot = here.astype(jnp.int32)[None]

    share, taps_share = norm_gain.shape[0], conv_query.size
    packed = jnp.concatenate(
        [norm_gain, ffn_gain]
        + [taps.reshape(-1) for taps in (conv_query, conv_key, conv_value)]
        + [head_gain]
    )
    row = lax.axis_index("row")
    packed = lax.dynamic_update_slice(
        jnp.zeros((ways * rows_ways, packed.shape[0]), BF), packed[None], (here * rows_ways + row, 0)
    )
    packed = sum_over(packed, "col", ways, 2)
    first_share = after(inputs[0], packed)
    packed = sum_over(sum_over(packed, "col", 2, 1, ways), "row", rows_ways)
    gain_one = packed[:, :share].reshape(1, width).astype(F32)
    gain_two = packed[:, share : 2 * share].reshape(1, width).astype(F32)
    mine = lax.dynamic_slice_in_dim(packed, here * rows_ways, rows_ways, axis=0).astype(F32)
    taps = mine[:, 2 * share : 2 * share + 3 * taps_share]
    taps = taps.reshape(rows_ways, 3, share, 4).transpose(3, 1, 0, 2).reshape(4, 3 * hw)
    taps = jnp.pad(taps, ((0, 4), (0, 0)))
    gain_head = mine[:, 2 * share + 3 * taps_share :].reshape(1, 128)
    own_one = lax.dynamic_slice_in_dim(gain_one, here * block, block, axis=1)
    own_two = lax.dynamic_slice_in_dim(gain_two, here * block, block, axis=1)

    beta_wide = jnp.pad(w_beta, ((0, 0), (0, 128 - heads)))
    qkv_share = jnp.concatenate([w_query, w_key, w_value, beta_wide], axis=1)
    qkv = lax.all_gather(qkv_share, "row", axis=0, tiled=False)
    out_parts = lax.all_gather(w_out, "row", axis=0, tiled=False)
    gates = lax.all_gather(w_gate.T, "row", axis=0, tiled=False)
    ups = lax.all_gather(w_up.T, "row", axis=0, tiled=False)
    down = lax.all_gather(w_down, "row", axis=0, tiled=False)

    data = [token_marks(segment[m].reshape(per, SEQ), CHUNK) for m in range(micro)]
    x_base, cot_near, mine = [], [], first_share
    for m in range(micro):
        near = gather_near(mine, ways)
        x_base.append(gather_far(near, ways))
        if m < micro - 1:
            mine = after(inputs[m + 1], arrays_of(near))
    for m in range(micro):
        mine = after(cotangent[m], arrays_of(x_base[-1]))
        cot_near.append(gather_near(mine, ways))
    cot_base = []
    weight = qkv.reshape(width, -1)
    pres, act_ones, inv_ones, mixed, saved = [], [], [], [], []
    resids, act_base = [], []

    def add_residual(m, own, arrived):
        resids.append(inputs[m].astype(F32) + total_of(own, arrived))
        near = gather_near(resids[m].astype(BF), ways)
        act_base.append(near if m else gather_far(near, ways, down))

    flying = None
    for m in range(micro):
        pieces = other_core(x_base[m], ways)
        if m:
            own, pairs = add_pairs(sums, send_pairs(sums, ways))
            flying = own, scatter_cols(pairs, ways)
            pieces = pieces_after(pieces, arrays_of(pairs))
        pre, act, stat = project(pieces, gain_one, weight, spot, block)
        if m:
            pre, cot_base[m - 1] = covered(pre, cot_base[m - 1])
            if m == micro - 1:
                pre, gates = lax.optimization_barrier((pre, gates))
        pres.append(pre.reshape(per, SEQ, -1))
        act_ones.append(act)
        inv_ones.append(stat[:, 0:1])
        array, rest = mix_forward(pres[m], data[m], taps, gain_head, heads)
        if m < micro - 1:
            cot_base.append(gather_far(cot_near[m], ways, array))
            array, x_base[m + 1] = covered(array, x_base[m + 1])
        else:
            array, cot_base[m] = covered(array, cot_base[m])
        mixed.append(array.reshape(tokens, hw))
        saved.append(rest)
        sums = spread(mixed[m], out_parts, spot, block, ways, False)
        if m == micro - 2:
            cot_base.append(gather_far(cot_near[m + 1], ways, sums))
        if flying:
            sums, arrived = covered(sums, flying[1])
            add_residual(m - 1, flying[0], arrived)
            sums = after(sums, resids[m - 1])
        if m == micro - 1:
            sums, ups = lax.optimization_barrier((sums, ups))
    own, pairs = add_pairs(sums, send_pairs(sums, ways))
    flying = own, scatter_cols(pairs, ways)
    cots = [other_core(base, ways) for base in cot_base]

    ffn_saved, ffn_outs, inners, resid_grads, grad_base = [], [], [], [], []
    down_grad, gate_grad, up_grad, gain_two_grad = None, None, None, 0.0

    def finish_ffn(m, own, arrived):
        inverse = ffn_saved[m][5][:, 0:1]
        act_grad = total_of(own, arrived)
        unit = resids[m] * inverse
        resid_grads.append(
            cotangent[m].astype(F32) + inverse * (act_grad * own_two - unit * inners[m])
        )
        grad_base.append(gather_near(resid_grads[m].astype(BF), ways))
        return jnp.sum(act_grad * unit, axis=0)

    for m in range(micro):
        pieces = other_core(act_base[m], ways)
        if m:
            pieces = pieces_after(pieces, up_grad, inners)
        else:
            pieces = pieces_after(pieces, arrays_of(pairs))
        kept, grads, outs = feed_forward(
            pieces, cots[m], gain_two, gates, ups, down, spot, block, ways, m == micro - 1
        )
        (kept, grads, outs), arrived = covered((kept, grads, outs), flying[1])
        if m < micro - 1:
            add_residual(m + 1, flying[0], arrived)
            kept, grads = after((kept, grads), resids[m + 1])
        else:
            gain_two_grad = gain_two_grad + finish_ffn(m - 1, flying[0], arrived)
            kept, grads = after((kept, grads), resid_grads[m - 1])
        if m:
            kept, ffn_outs[m - 1] = lax.optimization_barrier((kept, ffn_outs[m - 1]))
        ffn_saved.append(kept)
        inners.append(sum_cols(kept[5][:, 1], ways)[:, None] / width)
        last = m == micro - 1
        down_grad, arrived = covered(
            grow(down_grad, kept[2], kept[1], last), send_pairs(grads, ways)
        )
        own, pairs = add_pairs(grads, arrived)
        gate_grad = grow(gate_grad, kept[3], after(kept[0], arrays_of(pairs)), last)
        base = grad_base[0] if last else act_base[m + 1]
        gate_grad, base = covered(gate_grad, base)
        base = gather_far(base, ways)
        right = after(kept[0], gate_grad, inners[m])
        if last:
            gate_grad, arrived = covered(gate_grad, send_pairs(outs, ways))
            out_own, out_sums = add_pairs(outs, arrived)
            right = after(right, arrays_of(out_sums))
        else:
            ffn_outs.append(
                lax.psum_scatter(outs[0], "col", scatter_dimension=1, tiled=True)
            )
        up_grad, base = covered(grow(up_grad, kept[4], right, last), base)
        if not last:
            act_base[m + 1] = base
        flying = own, scatter_cols(pieces_after(pairs, arrays_of(base)), ways)
    pieces = other_core(base, ways)
    grad_down = scatter_row(down_grad, 1)
    grad_gate = scatter_row(gate_grad, 1)
    grad_up = scatter_row(up_grad, 1)

    qkv_terms, out_terms, firsts, dconv, dgain = [], [], [], 0.0, 0.0
    behind, stats = None, []
    for m in range(micro):
        whole, dao = collect(pieces, out_parts, spot, block, ways)
        if m == micro - 1:
            out_terms.append(dot_tn(mixed[m], whole))
            out_flying = scatter_cols(pieces_after(out_sums, arrays_of(pieces)), ways)
            grad_out = scatter_row(sum(out_terms), 1)
            dao = after(dao, out_terms)
        dpre, stat, dconv_part, dgain_part = mix_backward(
            pres[m], data[m], taps, gain_head, saved[m], dao.reshape(per, SEQ, hw), heads
        )
        dpre = dpre.reshape(tokens, -1)
        dconv, dgain = dconv + dconv_part, dgain + dgain_part
        if m == 0:
            dpre, grad_down = lax.optimization_barrier((dpre, grad_down))
        if flying:
            dpre, arrived = covered(dpre, flying[1])
            gain_two_grad = gain_two_grad + finish_ffn(micro - 1, flying[0], arrived)
            dpre, flying = after(dpre, resid_grads[-1]), None
        if behind:
            dpre, arrived = covered(dpre, behind[1])
            firsts.append((behind[0], arrived))
        if m < micro - 1:
            sums = spread(dpre, qkv, spot, block, ways, True)
            term, arrived = covered(
                dot_tn(act_ones[m], after(dpre, sums)), send_pairs(sums, ways)
            )
            stats.append(after(stat, sums))
            own, pairs = add_pairs(sums, arrived)
            term, base = covered(term, grad_base[m + 1])
            base = gather_far(base, ways)
            qkv_terms.append(term)
            out_term = dot_tn(mixed[m], after(whole, term, arrays_of(pairs)))
            out_term, base = covered(out_term, base)
            behind = own, scatter_cols(pieces_after(pairs, arrays_of(base)), ways)
            out_terms.append(out_term)
            pieces = pieces_after(other_core(base, ways), out_term)
        else:
            dpre, grad_gate, grad_up, grad_out = lax.optimization_barrier(
                (dpre, grad_gate, grad_up, grad_out)
            )
            qkv_grad = (sum(qkv_terms) + dot_tn(act_ones[m], dpre)).astype(BF)
            dpre = after(dpre, qkv_grad)
            grad_qkv = scatter_row(qkv_grad, 0)
            sums = spread(dpre, qkv, spot, block, ways, True)
            sums, flown = covered(sums, out_flying)
            arrived = send_pairs(sums, ways)
            totals = [
                resid + out.astype(F32) for resid, out in zip(resids[:-1], after(ffn_outs, sums))
            ] + [resids[-1] + total_of(out_own, flown)]
            outputs = [total.astype(BF) for total in totals]
            outputs, arrived = covered(outputs, arrived)
            own, pairs = add_pairs(sums, arrived)
            firsts.append((own, scatter_cols(pairs, ways, "split")))
            firsts[0] = after(firsts[0][0], arrays_of(pairs)), firsts[0][1]
            stat, dconv, dgain = after((stat, dconv, dgain), sums)
            stats.append(stat)
    means = [
        sum_cols(stat.reshape(tokens, 128)[:, 0], ways)[:, None] / width for stat in stats
    ]
    input_grads, gain_one_grad = [], 0.0
    for m in range(micro):
        act_grad = total_of(*firsts[m])
        unit = inputs[m].astype(F32) * inv_ones[m]
        gain_one_grad = gain_one_grad + jnp.sum(act_grad * unit, axis=0)
        input_grads.append(
            resid_grads[m] + inv_ones[m] * (act_grad * own_one - unit * means[m])
        )

    grad_qkv, grad_out, grad_gate, grad_up, grad_down = (
        grad.astype(F32) for grad in (grad_qkv, grad_out, grad_gate, grad_up, grad_down)
    )
    head_sum = sum_cols(jnp.sum(dgain, axis=0), ways)
    conv_sum = dconv.reshape(4, 8, 3, hw).sum(axis=1).transpose(1, 2, 0)
    early = sum_over(
        jnp.concatenate([conv_sum.reshape(-1), head_sum, gain_two_grad]), "row", rows_ways
    )
    late = sum_over(gain_one_grad, "row", rows_ways)
    conv_grads = lax.dynamic_slice_in_dim(
        early[: 12 * hw].reshape(3, hw, 4), row * share, share, axis=1
    )
    grad_head = lax.dynamic_slice_in_dim(
        early[12 * hw : 12 * hw + 128], row * head_gain.shape[0], head_gain.shape[0]
    )
    grad_two = lax.dynamic_slice_in_dim(early[12 * hw + 128 :], row * share, share)
    grad_one = lax.dynamic_slice_in_dim(late, row * share, share)
    return (
        jnp.stack(outputs),
        jnp.stack(input_grads),
        grad_one,
        grad_qkv[:, :hw],
        grad_qkv[:, hw : 2 * hw],
        grad_qkv[:, 2 * hw : 3 * hw],
        grad_qkv[:, 3 * hw : 3 * hw + heads],
        conv_grads[0],
        conv_grads[1],
        conv_grads[2],
        grad_head,
        grad_out,
        grad_two,
        grad_gate.T,
        grad_up.T,
        grad_down,
    )


def solution(mesh):
    both = P(("col", "row"))
    taps = P(("col", "row"), None)
    rows_cols, cols_rows = P("row", "col"), P("col", "row")
    tokens = P(None, "row", "col")
    in_specs = (
        tokens, tokens, P(None, "row"), both, rows_cols, rows_cols, rows_cols, rows_cols,
        taps, taps, taps, P("row"), cols_rows, both, rows_cols, rows_cols, cols_rows,
    )
    out_specs = (
        tokens, tokens, both, rows_cols, rows_cols, rows_cols, rows_cols,
        taps, taps, taps, P("row"), cols_rows, both, rows_cols, rows_cols, cols_rows,
    )
    body = partial(local, mesh.shape["col"], mesh.shape["row"])
    return jax.shard_map(body, mesh=mesh, in_specs=in_specs, out_specs=out_specs, check_vma=False)
```

```python
from functools import partial

import jax
import jax.numpy as jnp
from jax import lax
from jax.experimental import pallas as pl
from jax.experimental.pallas import tpu as pltpu
from jax.sharding import PartitionSpec as P

SEQ = 2048
CHUNK = 128
FWD_SUB = 4
BWD_SUB = 2
TILE = 512
HALO = 8
EPSILON = 1e-06
HEAD_FLOOR = 0.002
BF = jnp.bfloat16
F32 = jnp.float32
FFN_TILE = 256
PER_MICRO = 4.0e8


def dot_nn(a, b):
    return lax.dot_general(a, b, (((1,), (0,)), ((), ())), preferred_element_type=F32)


def dot_nt(a, b):
    return lax.dot_general(a, b, (((1,), (1,)), ((), ())), preferred_element_type=F32)


def dot_tn(a, b):
    return lax.dot_general(a, b, (((0,), (0,)), ((), ())), preferred_element_type=F32)


def token_marks(labels, chunk):
    seqs, length = labels.shape
    padded_back = jnp.pad(labels, ((0, 0), (4, 0)), constant_values=-1)
    padded_fore = jnp.pad(labels, ((0, 0), (0, 4)), constant_values=-2)
    marks = [labels]
    for lag in (1, 2, 3):
        marks.append(padded_back[:, 4 - lag : 4 - lag + length] == labels)
    for lag in (1, 2, 3):
        marks.append(padded_fore[:, lag : lag + length] == labels)
    grid = labels.reshape(seqs, length // chunk, chunk)
    prior = jnp.pad(grid[:, :-1, -1], ((0, 0), (1, 0)), constant_values=-1)
    marks.append((grid == prior[:, :, None]).reshape(seqs, length))
    marks.append((grid == grid[:, :, -1:]).reshape(seqs, length))
    marks.append(
        jnp.broadcast_to((grid[:, :, -1] == prior)[:, :, None], grid.shape).reshape(seqs, length)
    )
    marks += [jnp.zeros_like(labels)] * (16 - len(marks))
    marks = [mark.astype(F32).reshape(seqs, length // chunk, 1, chunk) for mark in marks]
    return jnp.concatenate(marks, axis=2)


LABEL, BACK, FORE, CARRIED, LAST, KEEP = 0, 0, 3, 7, 8, 9


def sigmoid(x):
    return 1.0 / (1.0 + jnp.exp(-x))


def level_marks(size):
    row = lax.broadcasted_iota(jnp.int32, (size, size), 0)
    col = lax.broadcasted_iota(jnp.int32, (size, size), 1)
    return row == col, row ^ col


def unit_lower_inverses(systems):
    size = systems[0].shape[0]
    diagonal, differ = level_marks(size)
    inverses = [
        (jnp.where(diagonal, 1.0, 0.0) - jnp.where(differ == 1, system, 0.0)).astype(BF)
        for system in systems
    ]
    block = 2
    while block < size:
        level = (differ >= block) & (differ < 2 * block)
        offs = [jnp.where(level, system, 0.0).astype(BF) for system in systems]
        lefts = [dot_nn(inverse, off).astype(BF) for inverse, off in zip(inverses, offs)]
        inverses = [
            inverse - dot_nn(left, inverse).astype(BF) for inverse, left in zip(inverses, lefts)
        ]
        block *= 2
    return inverses


def conv_rows(ext, taps, marks, lane, first, chunk):
    here = ext[pl.ds(HALO + first, chunk), lane]
    shifted = [here]
    total = here * taps[0:1, lane]
    for lag in (1, 2, 3):
        moved = ext[pl.ds(HALO + first - lag, chunk), lane] * marks[:, BACK + lag : BACK + lag + 1]
        shifted.append(moved)
        total = total + moved * taps[lag : lag + 1, lane]
    return total, shifted


def chunk_marks(marks_ref, seq, part, chunk):
    by_row = marks_ref[seq, part]
    marks = jnp.transpose(by_row)
    row = lax.broadcasted_iota(jnp.int32, (chunk, chunk), 0)
    col = lax.broadcasted_iota(jnp.int32, (chunk, chunk), 1)
    same = marks[:, LABEL : LABEL + 1] == by_row[LABEL : LABEL + 1, :]
    return (
        marks,
        same & (row > col),
        same & (row >= col),
        marks[:, CARRIED : CARRIED + 1],
        marks[:, LAST : LAST + 1],
        marks[0:1, KEEP : KEEP + 1],
    )


def mix_fwd_kernel(
    heads, chunk, sub, marks_ref, taps_ref, gain_ref, pre_ref,
    ao_ref, o_ref, u_ref, w_ref, state_ref, inv_ref, ext, memory,
):
    seqs = pre_ref.shape[0]
    wide = 3 * heads * 128
    size = sub * chunk

    @pl.when(pl.program_id(0) == 0)
    def _():
        ext[:, 0:HALO, :] = jnp.zeros((seqs, HALO, wide), F32)
        memory[...] = jnp.zeros_like(memory)

    ext[:, HALO : HALO + size, :] = pre_ref[:, :, 0:wide]
    kept = {
        (seq, part): chunk_marks(marks_ref, seq, part, chunk)
        for seq in range(seqs)
        for part in range(sub)
    }
    chains = [(seq, head) for seq in range(seqs) for head in range(heads)]
    units = [(seq, head, part) for part in range(sub) for seq, head in chains]
    boths, values, betas, attns, keys_list, systems = {}, {}, {}, {}, {}, {}
    for unit in units:
        seq, head, part = unit
        marks = kept[seq, part][0]
        acts = []
        for kind in range(3):
            lane = pl.ds((kind * heads + head) * 128, 128)
            cv, _ = conv_rows(ext.at[seq], taps_ref, marks, lane, part * chunk, chunk)
            acts.append(cv * sigmoid(cv))
        q1, k1, values[unit] = acts
        qn = q1 * (lax.rsqrt(jnp.sum(q1 * q1, axis=1, keepdims=True) + EPSILON) * 128 ** (-0.5))
        kn = k1 * lax.rsqrt(jnp.sum(k1 * k1, axis=1, keepdims=True) + EPSILON)
        betas[unit] = sigmoid(
            pre_ref[seq, part * chunk : (part + 1) * chunk, wide + head : wide + head + 1]
        )
        boths[unit] = jnp.concatenate([qn.astype(BF), kn.astype(BF)], axis=0)
    for unit in units:
        _, strict, within, _, _, _ = kept[unit[0], unit[2]]
        scores = dot_nt(boths[unit], boths[unit][chunk:])
        attns[unit] = jnp.where(within, scores[:chunk], 0.0).astype(BF)
        keys = jnp.where(strict, scores[chunk:], 0.0)
        keys_list[unit] = keys.astype(BF)
        systems[unit] = keys * betas[unit]
    inverses = dict(zip(units, unit_lower_inverses([systems[unit] for unit in units])))
    for part in range(sub):
        here = [(seq, head, part) for seq, head in chains]
        states = [memory[index] for index in range(len(here))]
        lows = [state.astype(BF) for state in states]
        seens = [dot_nn(boths[unit], low) for unit, low in zip(here, lows)]
        rights = [
            values[unit] - kept[unit[0], part][3] * seen[chunk:]
            for unit, seen in zip(here, seens)
        ]
        updates = [
            dot_nn(inverses[unit], (betas[unit] * right).astype(BF))
            for unit, right in zip(here, rights)
        ]
        for index, unit in enumerate(here):
            last, keep = kept[unit[0], part][4:]
            memory[index] = keep * states[index] + dot_tn(
                boths[unit][chunk:], (last * updates[index]).astype(BF)
            )
        for index, unit in enumerate(here):
            seq, head, _ = unit
            carried = kept[seq, part][3]
            rows = slice(part * chunk, (part + 1) * chunk)
            ub = updates[index].astype(BF)
            mixed = dot_nn(jnp.concatenate([attns[unit], keys_list[unit]], axis=0), ub)
            out = carried * seens[index][:chunk] + mixed[:chunk]
            wrong = rights[index] - mixed[chunk:]
            lane = pl.ds(head * 128, 128)
            scale = lax.rsqrt(jnp.maximum(jnp.mean(out * out, axis=1, keepdims=True), HEAD_FLOOR))
            ao_ref[seq, rows, lane] = (out * scale * gain_ref[...]).astype(BF)
            o_ref[seq, rows, lane] = out
            u_ref[seq, rows, lane] = ub
            w_ref[seq, rows, lane] = wrong.astype(BF)
            inv_ref[part, index] = inverses[unit]
            state_ref[part, index] = lows[index]
    ext[:, 0:HALO, :] = ext[:, size : size + HALO, :]


def mix_bwd_kernel(
    heads, chunk, sub, marks_ref, taps_ref, gain_ref,
    o_ref, u_ref, w_ref, state_ref, inv_ref, pre_ref, halo_ref, dao_ref,
    dpre_ref, stat_ref, dconv_ref, dgain_ref, ext, dext, memory,
):
    seqs = pre_ref.shape[0]
    wide = 3 * heads * 128
    size = sub * chunk

    @pl.when(pl.program_id(0) == 0)
    def _():
        dext[:, size : size + HALO, :] = jnp.zeros((seqs, HALO, wide), F32)
        memory[...] = jnp.zeros_like(memory)
        dconv_ref[...] = jnp.zeros_like(dconv_ref)
        dgain_ref[...] = jnp.zeros_like(dgain_ref)

    ext[:, 0:HALO, :] = halo_ref[:, :, 0:wide]
    ext[:, HALO : HALO + size, :] = pre_ref[:, :, 0:wide]
    gain = gain_ref[...]

    def fold(rows):
        return jnp.sum(rows.reshape(chunk // 8, 8, 128), axis=0)

    kept = {
        (seq, part): chunk_marks(marks_ref, seq, part, chunk)
        for seq in range(seqs)
        for part in range(sub)
    }
    chains = [(seq, head) for seq in range(seqs) for head in range(heads)]
    units = [(seq, head, part) for part in reversed(range(sub)) for seq, head in chains]

    def rows_of(unit):
        return slice(unit[2] * chunk, (unit[2] + 1) * chunk)

    def lane_of(unit, kind=0):
        return pl.ds((kind * heads + unit[1]) * 128, 128)

    acts, scales, norms, betas, boths, dobs, cdos = {}, {}, {}, {}, {}, {}, {}
    for unit in units:
        seq, head, part = unit
        marks, _, _, carried, _, _ = kept[seq, part]
        for kind in range(3):
            cv, _ = conv_rows(
                ext.at[seq], taps_ref, marks, lane_of(unit, kind), part * chunk, chunk
            )
            sg = sigmoid(cv)
            acts[unit, kind] = cv * sg
            scales[unit, kind] = sg * (1.0 + cv * (1.0 - sg))
        q1, k1 = acts[unit, 0], acts[unit, 1]
        rq = lax.rsqrt(jnp.sum(q1 * q1, axis=1, keepdims=True) + EPSILON)
        rk = lax.rsqrt(jnp.sum(k1 * k1, axis=1, keepdims=True) + EPSILON)
        norms[unit] = rq, rk
        boths[unit] = jnp.concatenate(
            [(q1 * (rq * 128 ** (-0.5))).astype(BF), (k1 * rk).astype(BF)], axis=0
        )
        betas[unit] = sigmoid(pre_ref[seq, rows_of(unit), wide + head : wide + head + 1])
        out = o_ref[seq, rows_of(unit), lane_of(unit)]
        square = jnp.mean(out * out, axis=1, keepdims=True)
        scale = lax.rsqrt(jnp.maximum(square, HEAD_FLOOR))
        ro = out * scale
        dao = dao_ref[seq, rows_of(unit), lane_of(unit)]
        dgain_ref[...] += fold(dao * ro)
        eo = dao * gain
        inner = jnp.mean(eo * ro, axis=1, keepdims=True)
        inner = jnp.where(square > HEAD_FLOOR, inner, 0.0)
        do = scale * (eo - ro * inner)
        dobs[unit] = do.astype(BF)
        cdos[unit] = (carried * do).astype(BF)
    firsts, grows, crosses = {}, {}, {}
    for unit in units:
        _, _, within, _, _, _ = kept[unit[0], unit[2]]
        both = boths[unit]
        attn = jnp.where(within, dot_nt(both[:chunk], both[chunk:]), 0.0).astype(BF)
        firsts[unit] = dot_tn(attn, dobs[unit])
        grows[unit] = dot_tn(both[:chunk], cdos[unit])
    drs, seconds, dbetas = {}, {}, {}
    for part in reversed(range(sub)):
        here = [(seq, head, part) for seq, head in chains]
        olds = [memory[index] for index in range(len(here))]
        lows = [old.astype(BF) for old in olds]
        fromstate = [dot_nn(boths[unit][chunk:], low) for unit, low in zip(here, lows)]
        dus = [
            (firsts[unit] + kept[unit[0], part][4] * term).astype(BF)
            for unit, term in zip(here, fromstate)
        ]
        drhs = [dot_tn(inv_ref[part, index], du) for index, du in enumerate(dus)]
        for index, unit in enumerate(here):
            drs[unit] = betas[unit] * drhs[index]
            carried, _, keep = kept[unit[0], part][3:]
            memory[index] = (
                keep * olds[index]
                + grows[unit]
                - dot_tn(boths[unit][chunk:], (carried * drs[unit]).astype(BF))
            )
        for index, unit in enumerate(here):
            wrong = w_ref[unit[0], rows_of(unit), lane_of(unit)].astype(F32)
            dbetas[unit] = jnp.sum(drhs[index] * wrong, axis=1, keepdims=True)
            seconds[unit] = dot_nt(u_ref[unit[0], rows_of(unit), lane_of(unit)], lows[index])
    shares = {}
    for unit in units:
        seq, head, part = unit
        marks, strict, within, carried, last, _ = kept[seq, part]
        both, kb = boths[unit], boths[unit][chunk:]
        index = seq * heads + head
        stack = jnp.concatenate([dobs[unit], drs[unit].astype(BF)], axis=0)
        right = jnp.concatenate(
            [u_ref[seq, rows_of(unit), lane_of(unit)], state_ref[part, index]], axis=0
        )
        cross = dot_nt(stack, right)
        dattn = jnp.where(within, cross[:chunk, :chunk], 0.0).astype(BF)
        dkeys = jnp.where(strict, -cross[chunk:, :chunk], 0.0).astype(BF)
        dboth = jnp.concatenate([dattn, dkeys], axis=0)
        by_row = dot_nn(dboth, kb)
        dqn = carried * cross[:chunk, chunk:] + by_row[:chunk]
        dkn = (
            dot_tn(dboth, both)
            + last * seconds[unit]
            + by_row[chunk:]
            - carried * cross[chunk:, chunk:]
        )
        (rq, rk), q1, k1 = norms[unit], acts[unit, 0], acts[unit, 1]
        dq1 = 128 ** (-0.5) * rq * (
            dqn - (rq * rq) * q1 * jnp.sum(q1 * dqn, axis=1, keepdims=True)
        )
        dk1 = rk * (dkn - (rk * rk) * k1 * jnp.sum(k1 * dkn, axis=1, keepdims=True))
        for kind, dact in enumerate((dq1, dk1, drs[unit])):
            dext[seq, rows_of(unit), lane_of(unit, kind)] = dact * scales[unit, kind]
    for unit in units:
        seq, head, part = unit
        marks = kept[seq, part][0]
        share = shares.get((seq, part), 0.0)
        for kind in range(3):
            lane = lane_of(unit, kind)
            _, shifts = conv_rows(ext.at[seq], taps_ref, marks, lane, part * chunk, chunk)
            dc = dext[seq, rows_of(unit), lane]
            back = dc * taps_ref[0:1, lane]
            dconv_ref[0:8, lane] += fold(dc * shifts[0])
            for lag in (1, 2, 3):
                dconv_ref[8 * lag : 8 * lag + 8, lane] += fold(dc * shifts[lag])
                back = back + (
                    dext[seq, pl.ds(part * chunk + lag, chunk), lane]
                    * marks[:, FORE + lag : FORE + lag + 1]
                    * taps_ref[lag : lag + 1, lane]
                )
            dpre_ref[seq, rows_of(unit), lane] = back.astype(BF)
            share = share + back * shifts[0]
        shares[seq, part] = share
    column = lax.broadcasted_iota(jnp.int32, (chunk, 128), 1)
    for seq, part in kept:
        rows = slice(part * chunk, (part + 1) * chunk)
        total = jnp.zeros((chunk, 128), F32)
        for head in range(heads):
            unit = seq, head, part
            grad = dbetas[unit] * betas[unit] * (1.0 - betas[unit])
            total = jnp.where(column == head, grad, total)
        dpre_ref[seq, rows, pl.ds(wide, 128)] = total.astype(BF)
        share = shares[seq, part] + total * pre_ref[seq, rows, pl.ds(wide, 128)]
        stat_ref[seq, rows] = jnp.broadcast_to(
            jnp.sum(share, axis=1, keepdims=True), (chunk, 128)
        )
    dext[:, size : size + HALO, :] = dext[:, 0:HALO, :]


def params():
    return pltpu.CompilerParams(dimension_semantics=("arbitrary",), vmem_limit_bytes=60 * 2**20)


def fixed(array):
    zeros = (0,) * array.ndim
    return pl.BlockSpec(array.shape, lambda n: zeros, pipeline_mode=pl.Buffered(1))


def cost(micros):
    return pl.CostEstimate(flops=int(micros * PER_MICRO), bytes_accessed=0, transcendentals=0)


def shape(dims, dtype):
    return jax.ShapeDtypeStruct(dims, dtype)


def mix_forward(pre, marks, taps, gain, heads, chunk=CHUNK, sub=FWD_SUB):
    seqs, length, cols = pre.shape
    chains, parts = seqs * heads, length // chunk
    steps = parts // sub
    wide, hw = 3 * heads * 128, heads * 128

    def tok(width):
        return pl.BlockSpec((seqs, sub * chunk, width), lambda n: (0, n, 0))

    out_shape = [
        shape((seqs, length, hw), BF),
        shape((seqs, length, hw), F32),
        shape((seqs, length, hw), BF),
        shape((seqs, length, hw), BF),
        shape((parts, chains, 128, 128), BF),
        shape((parts, chains, chunk, chunk), BF),
    ]
    mixed, *saved = pl.pallas_call(
        partial(mix_fwd_kernel, heads, chunk, sub),
        grid=(steps,),
        in_specs=[
            pl.BlockSpec((seqs, sub, 16, chunk), lambda n: (0, n, 0, 0)),
            fixed(taps), fixed(gain), tok(cols),
        ],
        out_specs=[tok(hw)] * 4 + [
            pl.BlockSpec((sub, chains, 128, 128), lambda n: (n, 0, 0, 0)),
            pl.BlockSpec((sub, chains, chunk, chunk), lambda n: (n, 0, 0, 0)),
        ],
        out_shape=out_shape,
        scratch_shapes=[
            pltpu.VMEM((seqs, HALO + sub * chunk, wide), F32),
            pltpu.VMEM((chains, 128, 128), F32),
        ],
        compiler_params=params(),
        cost_estimate=cost(24),
        name="mix_forward",
    )(marks, taps, gain, pre)
    return mixed, saved


def mix_backward(pre, marks, taps, gain, saved, dao, heads, chunk=CHUNK, sub=BWD_SUB):
    seqs, length, cols = pre.shape
    chains, parts = seqs * heads, length // chunk
    steps = parts // sub
    wide, hw = 3 * heads * 128, heads * 128
    end, groups = steps - 1, sub * chunk // HALO

    def tok(width):
        return pl.BlockSpec((seqs, sub * chunk, width), lambda n: (0, end - n, 0))

    halo = pl.BlockSpec(
        (seqs, HALO, cols), lambda n: (0, jnp.maximum((end - n) * groups - 1, 0), 0)
    )
    out_shape = [
        shape((seqs, length, cols), BF), shape((seqs, length, 128), F32),
        shape((32, wide), F32), shape((8, 128), F32),
    ]
    return pl.pallas_call(
        partial(mix_bwd_kernel, heads, chunk, sub),
        grid=(steps,),
        in_specs=[
            pl.BlockSpec((seqs, sub, 16, chunk), lambda n: (0, end - n, 0, 0)),
            fixed(taps), fixed(gain),
        ] + [tok(hw)] * 3 + [
            pl.BlockSpec((sub, chains, 128, 128), lambda n: (end - n, 0, 0, 0)),
            pl.BlockSpec((sub, chains, chunk, chunk), lambda n: (end - n, 0, 0, 0)),
            tok(cols), halo, tok(hw),
        ],
        out_specs=[
            tok(cols), tok(128),
            pl.BlockSpec((32, wide), lambda n: (0, 0)),
            pl.BlockSpec((8, 128), lambda n: (0, 0)),
        ],
        out_shape=out_shape,
        scratch_shapes=[
            pltpu.VMEM((seqs, HALO + sub * chunk, wide), F32),
            pltpu.VMEM((seqs, HALO + sub * chunk, wide), F32),
            pltpu.VMEM((chains, 128, 128), F32),
        ],
        compiler_params=params(),
        cost_estimate=cost(34),
        name="mix_backward",
    )(marks, taps, gain, *saved, pre, pre, dao)


def swap(values, bit, ways):
    return lax.ppermute(values, "col", [(i, i ^ bit) for i in range(ways)])


def gather_near(values, ways):
    base = [(0, 0, values)]
    if ways == 8:
        return base + [(far, 0, swap(values, far, ways)) for far in (2, 4)]
    bit = 2
    while bit < ways:
        base += [(far ^ bit, lane, swap(array, bit, ways)) for far, lane, array in base]
        bit *= 2
    return base


def gather_far(base, ways, *others):
    if ways != 8:
        return base
    along, across = base[1][2], base[2][2]
    half = along.shape[-1] // 2
    first, second = across[..., :half], along[..., half:]
    if others:
        first, second = after((first, second), others)
    return base + [(6, 0, swap(first, 2, ways)), (6, half, swap(second, 4, ways))]


def gather_cols(values, ways, way="direct"):
    base = gather_near(values, ways)
    if ways != 8 or way == "split":
        return gather_far(base, ways)
    return base + [(6, 0, swap(values, 6, ways))]


def other_core(base, ways):
    return base + [(far ^ 1, lane, swap(array, 1, ways)) for far, lane, array in base]


def after(values, *others):
    return lax.optimization_barrier((values, others))[0]


def arrays_of(pieces):
    return [array for _, _, array in pieces]


def pieces_after(pieces, *others):
    arrays = after(arrays_of(pieces), *others)
    return [(far, lane, array) for (far, lane, _), array in zip(pieces, arrays)]


def covered(results, pieces):
    results, arrays = lax.optimization_barrier((results, arrays_of(pieces)))
    return results, [(far, lane, array) for (far, lane, _), array in zip(pieces, arrays)]


def add_low(*terms):
    return sum(term.astype(F32) for term in terms).astype(BF)


def send_pairs(pieces, ways):
    return [(far, 0, swap(pieces[far | 1], 1, ways)) for far in range(0, ways, 2)]


def add_pairs(pieces, arrived):
    sums = [(far, 0, add_low(pieces[far], array)) for far, _, array in arrived if far]
    return (pieces[0], arrived[0][2]), sums


def scatter_cols(sums, ways, way="direct"):
    held = {far: array for far, _, array in sums}
    if ways == 8 and way == "direct":
        return [(far, 0, swap(held[far], far, ways)) for far in (2, 4, 6)]
    if ways == 8:
        half = held[2].shape[-1] // 2
        left = swap(held[6][..., :half], 2, ways)
        right = swap(held[6][..., half:], 4, ways)
        four = jnp.concatenate(
            [add_low(left, held[4][..., :half]), held[4][..., half:]], axis=-1
        )
        two = jnp.concatenate(
            [held[2][..., :half], add_low(right, held[2][..., half:])], axis=-1
        )
        return [(2, 0, swap(two, 2, ways)), (4, 0, swap(four, 4, ways))]
    terms = {far: (array,) for far, array in held.items()}
    terms[0] = ()
    bit = 2
    while bit < ways:
        terms = {
            far: terms[far] + (swap(add_low(*terms[far | bit]), bit, ways),)
            for far in terms
            if not far & bit
        }
        bit *= 2
    return [(0, 0, array) for array in terms[0]]


def total_of(own, arrived):
    return sum(array.astype(F32) for array in (*own, *arrays_of(arrived)))


def sum_over(values, axis, ways, bit=1, size=None):
    size = ways if size is None else size
    while bit < ways:
        values = values + lax.ppermute(values, axis, [(i, i ^ bit) for i in range(size)])
        bit *= 2
    return values


def sum_cols(values, ways):
    values = values + swap(values, 1, ways)
    return values + sum(swap(values, far, ways) for far in range(2, ways, 2))


def whole_blocks(layout, pieces):
    blocks = {}
    for (far, _), piece in zip(layout, pieces):
        blocks.setdefault(far, []).append(piece[...])
    return {
        far: parts[0] if len(parts) == 1 else jnp.concatenate(parts, axis=1)
        for far, parts in blocks.items()
    }


def lanes_of(spot_ref, far, block):
    return pl.ds(pl.multiple_of((spot_ref[0] ^ far) * block, block), block)


def part_of(spot_ref, far, block, step):
    index, each = spot_ref[0] ^ far, step // block
    return index // each, pl.ds(pl.multiple_of((index % each) * block, block), block)


def normed(blocks, spot_ref, gain_ref, act_ref, block):
    width = act_ref.shape[1]
    total = 0.0
    for rows in blocks.values():
        rows = rows.astype(F32)
        total = total + jnp.sum(rows * rows, axis=1, keepdims=True)
    inverse = lax.rsqrt(total / width + EPSILON)
    acts = {}
    for far, rows in blocks.items():
        lanes = lanes_of(spot_ref, far, block)
        acts[far] = (rows.astype(F32) * inverse * gain_ref[0:1, lanes]).astype(BF)
        act_ref[:, lanes] = acts[far]
    return acts, inverse


def project_kernel(layout, block, spot_ref, gain_ref, weight_ref, *refs):
    pieces, (pre_ref, act_ref, stat_ref) = refs[: len(layout)], refs[len(layout) :]
    blocks = whole_blocks(layout, pieces)
    acts, inverse = normed(blocks, spot_ref, gain_ref, act_ref, block)
    stat_ref[...] = jnp.broadcast_to(inverse, stat_ref.shape)
    total = 0.0
    for far, act in acts.items():
        total = total + dot_nn(act, weight_ref[lanes_of(spot_ref, far, block), :])
    pre_ref[...] = total


def spread_kernel(transposed, block, spot_ref, weight_ref, rows_ref, *outs):
    rows = rows_ref[...]
    step = weight_ref.shape[1 if transposed else 2]
    for far, out in enumerate(outs):
        part, lanes = part_of(spot_ref, far, block, step)
        if transposed:
            out[...] = dot_nt(rows, weight_ref[part, lanes, :]).astype(BF)
        else:
            out[...] = dot_nn(rows, weight_ref[part, :, lanes]).astype(BF)


def collect_kernel(layout, block, spot_ref, weight_ref, *refs):
    pieces, (whole_ref, out_ref) = refs[: len(layout)], refs[len(layout) :]
    for far, rows in whole_blocks(layout, pieces).items():
        whole_ref[:, lanes_of(spot_ref, far, block)] = rows
    step = weight_ref.shape[2]
    total = 0.0
    for part in range(weight_ref.shape[0]):
        total = total + dot_nt(
            whole_ref[:, part * step : (part + 1) * step], weight_ref[part]
        )
    out_ref[...] = total


def ffn_kernel(layout, cot_layout, block, ways, spot_ref, gain_ref, gates_ref, ups_ref, down_ref, *refs):
    count, total = len(layout), len(layout) + len(cot_layout)
    acts, cots, refs = refs[:count], refs[count:total], refs[total:]
    act_ref, cot_ref, hid_ref, dgate_ref, dup_ref, stat_ref = refs[:6]
    grads, outs = refs[6 : 6 + ways], refs[6 + ways : -4]
    whole, gates, ups, downs = refs[-4:]

    @pl.when(pl.program_id(0) == 0)
    def _():
        step = down_ref.shape[2]
        for part in range(down_ref.shape[0]):
            lanes = slice(part * step, (part + 1) * step)
            gates[:, lanes] = gates_ref[part]
            ups[:, lanes] = ups_ref[part]
            downs[:, lanes] = down_ref[part]

    for far, rows in whole_blocks(cot_layout, cots).items():
        cot_ref[:, lanes_of(spot_ref, far, block)] = rows
    _, inverse = normed(whole_blocks(layout, acts), spot_ref, gain_ref, act_ref, block)
    dhid = dot_nt(cot_ref[...], downs[...])
    gate = dot_nt(act_ref[...], gates[...])
    up = dot_nt(act_ref[...], ups[...])
    sig = sigmoid(gate)
    swish = gate * sig
    hid = (swish * up).astype(BF)
    dgate = (dhid * up * sig * (1.0 + gate * (1.0 - sig))).astype(BF)
    dup = (dhid * swish).astype(BF)
    hid_ref[...] = hid
    dgate_ref[...] = dgate
    dup_ref[...] = dup
    inner = jnp.sum(dgate.astype(F32) * gate + dup.astype(F32) * up, axis=1, keepdims=True)
    lane = lax.broadcasted_iota(jnp.int32, stat_ref.shape, 1)
    stat_ref[...] = jnp.where(lane == 0, inverse, inner)
    whole[...] = (dot_nn(dgate, gates[...]) + dot_nn(dup, ups[...])).astype(BF)
    for far, grad in enumerate(grads):
        grad[...] = whole[:, lanes_of(spot_ref, far, block)]
    if len(outs) == 1:
        outs[0][...] = dot_nn(hid, downs[...]).astype(BF)
    else:
        whole[...] = dot_nn(hid, downs[...]).astype(BF)
        for far, out in enumerate(outs):
            out[...] = whole[:, lanes_of(spot_ref, far, block)]


SPOT = pl.BlockSpec(memory_space=pltpu.SMEM)


def rows_spec(width, tile):
    return pl.BlockSpec((tile, width), lambda n: (n, 0))


def tiled(kernel, name, fixed_args, row_args, out_shape, tile, micros, spot, scratch=()):
    rows = row_args[0].shape[0]
    return pl.pallas_call(
        kernel,
        grid=(rows // tile,),
        in_specs=[SPOT]
        + [fixed(a) for a in fixed_args]
        + [rows_spec(a.shape[1], tile) for a in row_args],
        out_specs=[rows_spec(a.shape[1], tile) for a in out_shape],
        out_shape=out_shape,
        scratch_shapes=list(scratch),
        compiler_params=params(),
        cost_estimate=cost(micros),
        name=name,
    )(spot, *fixed_args, *row_args)


def layout_of(pieces):
    return tuple((far, lane) for far, lane, _ in pieces), [array for _, _, array in pieces]


def project(pieces, gain, weight, spot, block):
    layout, arrays = layout_of(pieces)
    rows, (width, cols) = arrays[0].shape[0], weight.shape
    out = [shape((rows, cols), F32), shape((rows, width), BF), shape((rows, 128), F32)]
    return tiled(
        partial(project_kernel, layout, block), "project", [gain, weight], arrays, out,
        TILE, 19, spot,
    )


def spread(rows_in, weight, spot, block, ways, transposed):
    rows = rows_in.shape[0]
    return tiled(
        partial(spread_kernel, transposed, block), "spread", [weight], [rows_in],
        [shape((rows, block), BF)] * ways, TILE, 14 if transposed else 7, spot,
    )


def collect(pieces, weight, spot, block, ways):
    layout, arrays = layout_of(pieces)
    rows = arrays[0].shape[0]
    out = [shape((rows, block * ways), BF), shape((rows, weight.shape[1]), F32)]
    return tiled(
        partial(collect_kernel, layout, block), "collect", [weight], arrays, out,
        TILE, 9, spot,
    )


def feed_forward(acts, cots, gain, gates, ups, down, spot, block, ways, split):
    layout, act_arrays = layout_of(acts)
    cot_layout, cot_arrays = layout_of(cots)
    rows, width, hidden = act_arrays[0].shape[0], block * ways, down.shape[1]
    out = (
        [shape((rows, width), BF)] * 2
        + [shape((rows, hidden), BF)] * 3
        + [shape((rows, 128), F32)]
        + [shape((rows, block), BF)] * ways
        + ([shape((rows, block), BF)] * ways if split else [shape((rows, width), BF)])
    )
    results = tiled(
        partial(ffn_kernel, layout, cot_layout, block, ways), "feed_forward", [gain, gates, ups, down],
        act_arrays + cot_arrays, out, FFN_TILE, 54, spot,
        [pltpu.VMEM((FFN_TILE, width), BF)] + [pltpu.VMEM((hidden, width), BF)] * 3,
    )
    return results[:6], results[6 : 6 + ways], results[6 + ways :]


def outer(lefts, rights):
    total = None
    for left, right in zip(lefts, rights):
        term = dot_tn(left, right)
        total = term if total is None else total + term
    return total


def grow(total, left, right, last):
    term = dot_tn(left, right)
    term = term if total is None else total + term
    return term.astype(BF) if last else term


def scatter_row(values, dim):
    return lax.psum_scatter(
        values.astype(BF), "row", scatter_dimension=dim, tiled=True
    )


def local(
    ways, rows_ways, inputs, cotangent, segment, norm_gain, w_query, w_key, w_value, w_beta,
    conv_query, conv_key, conv_value, head_gain, w_out, ffn_gain, w_gate, w_up, w_down,
):
    micro, tokens, block = inputs.shape
    width = block * ways
    heads = w_beta.shape[1]
    hw = heads * 128
    per = tokens // SEQ
    here = lax.axis_index("col")
    spot = here.astype(jnp.int32)[None]

    share, taps_share = norm_gain.shape[0], conv_query.size
    packed = jnp.concatenate(
        [norm_gain, ffn_gain]
        + [taps.reshape(-1) for taps in (conv_query, conv_key, conv_value)]
        + [head_gain]
    )
    row = lax.axis_index("row")
    packed = lax.dynamic_update_slice(
        jnp.zeros((ways * rows_ways, packed.shape[0]), BF), packed[None], (here * rows_ways + row, 0)
    )
    packed = sum_over(packed, "col", ways, 2)
    first_share = after(inputs[0], packed)
    packed = sum_over(sum_over(packed, "col", 2, 1, ways), "row", rows_ways)
    gain_one = packed[:, :share].reshape(1, width).astype(F32)
    gain_two = packed[:, share : 2 * share].reshape(1, width).astype(F32)
    mine = lax.dynamic_slice_in_dim(packed, here * rows_ways, rows_ways, axis=0).astype(F32)
    taps = mine[:, 2 * share : 2 * share + 3 * taps_share]
    taps = taps.reshape(rows_ways, 3, share, 4).transpose(3, 1, 0, 2).reshape(4, 3 * hw)
    taps = jnp.pad(taps, ((0, 4), (0, 0)))
    gain_head = mine[:, 2 * share + 3 * taps_share :].reshape(1, 128)
    own_one = lax.dynamic_slice_in_dim(gain_one, here * block, block, axis=1)
    own_two = lax.dynamic_slice_in_dim(gain_two, here * block, block, axis=1)

    beta_wide = jnp.pad(w_beta, ((0, 0), (0, 128 - heads)))
    qkv_share = jnp.concatenate([w_query, w_key, w_value, beta_wide], axis=1)
    qkv = lax.all_gather(qkv_share, "row", axis=0, tiled=False)
    out_parts = lax.all_gather(w_out, "row", axis=0, tiled=False)
    gates = lax.all_gather(w_gate.T, "row", axis=0, tiled=False)
    ups = lax.all_gather(w_up.T, "row", axis=0, tiled=False)
    down = lax.all_gather(w_down, "row", axis=0, tiled=False)

    data = [token_marks(segment[m].reshape(per, SEQ), CHUNK) for m in range(micro)]
    x_base, cot_near, mine = [], [], first_share
    for m in range(micro):
        near = gather_near(mine, ways)
        x_base.append(gather_far(near, ways))
        if m < micro - 1:
            mine = after(inputs[m + 1], arrays_of(near))
    for m in range(micro):
        mine = after(cotangent[m], arrays_of(x_base[-1]))
        cot_near.append(gather_near(mine, ways))
    cot_base = []
    weight = qkv.reshape(width, -1)
    pres, act_ones, inv_ones, mixed, saved = [], [], [], [], []
    resids, act_base = [], []

    def add_residual(m, own, arrived):
        resids.append(inputs[m].astype(F32) + total_of(own, arrived))
        if m:
            act_base.append(gather_cols(resids[m].astype(BF), ways))
            return
        near = gather_near(resids[m].astype(BF), ways)
        act_base.append(gather_far(near, ways))

    flying = None
    for m in range(micro):
        pieces = other_core(x_base[m], ways)
        if m:
            own, pairs = add_pairs(sums, send_pairs(sums, ways))
            flying = own, scatter_cols(pairs, ways)
            pieces = pieces_after(pieces, arrays_of(pairs))
        pre, act, stat = project(pieces, gain_one, weight, spot, block)
        if m:
            pre, cot_base[m - 1] = covered(pre, cot_base[m - 1])
            if m == micro - 1:
                pre, gates = lax.optimization_barrier((pre, gates))
        pres.append(pre.reshape(per, SEQ, -1))
        act_ones.append(act)
        inv_ones.append(stat[:, 0:1])
        array, rest = mix_forward(pres[m], data[m], taps, gain_head, heads)
        if m < micro - 1:
            cot_base.append(gather_far(cot_near[m], ways, array))
            array, x_base[m + 1] = covered(array, x_base[m + 1])
        else:
            array, cot_base[m] = covered(array, cot_base[m])
        mixed.append(array.reshape(tokens, hw))
        saved.append(rest)
        sums = spread(mixed[m], out_parts, spot, block, ways, False)
        if m == micro - 2:
            cot_base.append(gather_far(cot_near[m + 1], ways, sums))
        if flying:
            sums, arrived = covered(sums, flying[1])
            add_residual(m - 1, flying[0], arrived)
            sums = after(sums, resids[m - 1])
        if m == micro - 1:
            sums, ups = lax.optimization_barrier((sums, ups))
    own, pairs = add_pairs(sums, send_pairs(sums, ways))
    arrived = scatter_cols(pairs, ways, "split")
    add_residual(micro - 1, own, arrived)
    cots = [other_core(base, ways) for base in cot_base]

    ffn_saved, ffn_outs, inners, resid_grads, grad_base = [], [], [], [], []
    down_grad, gate_grad, up_grad, gain_two_grad = None, None, None, 0.0

    def finish_ffn(m, own, arrived):
        inverse = ffn_saved[m][5][:, 0:1]
        act_grad = total_of(own, arrived)
        unit = resids[m] * inverse
        resid_grads.append(
            cotangent[m].astype(F32) + inverse * (act_grad * own_two - unit * inners[m])
        )
        grad_base.append(gather_near(resid_grads[m].astype(BF), ways))
        return jnp.sum(act_grad * unit, axis=0)

    flying = None
    for m in range(micro):
        last = m == micro - 1
        pieces = other_core(act_base[m], ways)
        pieces = pieces_after(pieces, resids, down_grad, arrays_of(pairs))
        kept, grads, outs = feed_forward(
            pieces, cots[m], gain_two, gates, ups, down, spot, block, ways, last
        )
        if not last:
            (kept, grads, outs), act_base[m + 1] = covered(
                (kept, grads, outs), act_base[m + 1]
            )
        if flying:
            before = ffn_saved[m - 1]
            left = after(before[0], kept[5])
            gate_grad = grow(gate_grad, before[3], left, False)
            up_grad = grow(up_grad, before[4], after(left, gate_grad), False)
            (kept, grads, outs, gate_grad, up_grad), arrived = covered(
                (kept, grads, outs, gate_grad, up_grad), flying[1]
            )
            gain_two_grad = gain_two_grad + finish_ffn(m - 1, flying[0], arrived)
            kept, grads, ffn_outs[m - 1] = lax.optimization_barrier(
                (kept, after(grads, resid_grads[m - 1]), ffn_outs[m - 1])
            )
        ffn_saved.append(kept)
        inners.append(sum_cols(kept[5][:, 1], ways)[:, None] / width)
        down_grad, arrived = covered(
            grow(down_grad, kept[2], kept[1], last), send_pairs(grads, ways)
        )
        own, pairs = add_pairs(grads, arrived)
        if not last:
            flying = own, scatter_cols(pairs, ways)
            ffn_outs.append(
                lax.psum_scatter(outs[0], "col", scatter_dimension=1, tiled=True)
            )
    kept = ffn_saved[-1]
    gate_grad = grow(gate_grad, kept[3], after(kept[0], arrays_of(pairs)), True)
    gate_grad, arrived = covered(gate_grad, send_pairs(outs, ways))
    gate_grad, base = covered(gate_grad, grad_base[0])
    out_own, out_sums = add_pairs(outs, arrived)
    base = gather_far(base, ways)
    right = after(kept[0], gate_grad, arrays_of(out_sums))
    up_grad, base = covered(grow(up_grad, kept[4], right, True), base)
    flying = own, scatter_cols(pieces_after(pairs, arrays_of(base)), ways)
    pieces = other_core(base, ways)
    grad_down = scatter_row(down_grad, 1)
    grad_gate = scatter_row(gate_grad, 1)
    grad_up = scatter_row(up_grad, 1)

    qkv_terms, out_terms, firsts, dconv, dgain = [], [], [], 0.0, 0.0
    behind, means = None, []
    for m in range(micro):
        whole, dao = collect(pieces, out_parts, spot, block, ways)
        if m == micro - 1:
            out_terms.append(dot_tn(mixed[m], whole))
            out_flying = scatter_cols(pieces_after(out_sums, arrays_of(pieces)), ways)
            grad_out = scatter_row(sum(out_terms), 1)
            dao = after(dao, out_terms)
        dpre, stat, dconv_part, dgain_part = mix_backward(
            pres[m], data[m], taps, gain_head, saved[m], dao.reshape(per, SEQ, hw), heads
        )
        dpre = dpre.reshape(tokens, -1)
        dconv, dgain = dconv + dconv_part, dgain + dgain_part
        if m == 0:
            dpre, grad_down = lax.optimization_barrier((dpre, grad_down))
        if flying:
            dpre, arrived = covered(dpre, flying[1])
            gain_two_grad = gain_two_grad + finish_ffn(micro - 1, flying[0], arrived)
            dpre, flying = after(dpre, resid_grads[-1]), None
        if behind:
            dpre, arrived = covered(dpre, behind[1])
            firsts.append((behind[0], arrived))
        if m < micro - 1:
            sums = spread(dpre, qkv, spot, block, ways, True)
            term, arrived = covered(
                dot_tn(act_ones[m], after(dpre, sums)), send_pairs(sums, ways)
            )
            means.append(sum_cols(stat.reshape(tokens, 128)[:, 0], ways)[:, None] / width)
            own, pairs = add_pairs(sums, arrived)
            term, base = covered(term, grad_base[m + 1])
            base = gather_far(base, ways)
            qkv_terms.append(term)
            out_term = dot_tn(mixed[m], after(whole, term, arrays_of(pairs)))
            out_term, base = covered(out_term, base)
            behind = own, scatter_cols(pieces_after(pairs, arrays_of(base)), ways)
            out_terms.append(out_term)
            pieces = pieces_after(other_core(base, ways), out_term)
        else:
            dpre, grad_gate, grad_up, grad_out, means = lax.optimization_barrier(
                (dpre, grad_gate, grad_up, grad_out, means)
            )
            qkv_grad = (sum(qkv_terms) + dot_tn(act_ones[m], dpre)).astype(BF)
            dpre = after(dpre, qkv_grad)
            dconv, dgain, gain_two_grad = after((dconv, dgain, gain_two_grad), qkv_grad)
            conv_sum = dconv.reshape(4, 8, 3, hw).sum(axis=1).transpose(1, 2, 0)
            early = sum_over(
                jnp.concatenate(
                    [conv_sum.reshape(-1), jnp.sum(dgain, axis=0), gain_two_grad]
                ),
                "row", rows_ways,
            )
            grad_qkv = scatter_row(qkv_grad, 0)
            sums = spread(dpre, qkv, spot, block, ways, True)
            arrived = send_pairs(sums, ways)
            sums, flown = covered(sums, out_flying)
            own, pairs = add_pairs(sums, arrived)
            late_resids = after(resids, arrays_of(pairs))
            outputs = [
                (resid + out.astype(F32)).astype(BF)
                for resid, out in zip(late_resids[:-1], ffn_outs)
            ] + [(late_resids[-1] + total_of(out_own, flown)).astype(BF)]
            arrived = scatter_cols(pairs, ways, "split")
            firsts[0] = after(firsts[0][0], arrays_of(pairs)), firsts[0][1]
            stat, early = after((stat, early), arrays_of(pairs))
            means.append(sum_cols(stat.reshape(tokens, 128)[:, 0], ways)[:, None] / width)
            head_sum = sum_cols(early[12 * hw : 12 * hw + 128], ways)
    conv_grads = lax.dynamic_slice_in_dim(
        early[: 12 * hw].reshape(3, hw, 4), row * share, share, axis=1
    )
    grad_two = lax.dynamic_slice_in_dim(early[12 * hw + 128 :], row * share, share)
    output, conv_grads, grad_two = lax.optimization_barrier(
        (jnp.stack(outputs), [conv_grads[kind] for kind in range(3)], grad_two)
    )
    firsts.append((own, pieces_after(arrived, output, conv_grads, grad_two)))
    input_grads, gain_one_grad = [], 0.0
    for m in range(micro):
        act_grad = total_of(*firsts[m])
        unit = inputs[m].astype(F32) * inv_ones[m]
        gain_one_grad = gain_one_grad + jnp.sum(act_grad * unit, axis=0)
        input_grads.append(
            resid_grads[m] + inv_ones[m] * (act_grad * own_one - unit * means[m])
        )

    grad_qkv, grad_out, grad_gate, grad_up, grad_down = (
        grad.astype(F32) for grad in (grad_qkv, grad_out, grad_gate, grad_up, grad_down)
    )
    late = sum_over(gain_one_grad, "row", rows_ways)
    grad_head = lax.dynamic_slice_in_dim(
        head_sum, row * head_gain.shape[0], head_gain.shape[0]
    )
    grad_one = lax.dynamic_slice_in_dim(late, row * share, share)
    return (
        output,
        jnp.stack(input_grads),
        grad_one,
        grad_qkv[:, :hw],
        grad_qkv[:, hw : 2 * hw],
        grad_qkv[:, 2 * hw : 3 * hw],
        grad_qkv[:, 3 * hw : 3 * hw + heads],
        conv_grads[0],
        conv_grads[1],
        conv_grads[2],
        grad_head,
        grad_out,
        grad_two,
        grad_gate.T,
        grad_up.T,
        grad_down,
    )


def solution(mesh):
    both = P(("col", "row"))
    taps = P(("col", "row"), None)
    rows_cols, cols_rows = P("row", "col"), P("col", "row")
    tokens = P(None, "row", "col")
    in_specs = (
        tokens, tokens, P(None, "row"), both, rows_cols, rows_cols, rows_cols, rows_cols,
        taps, taps, taps, P("row"), cols_rows, both, rows_cols, rows_cols, cols_rows,
    )
    out_specs = (
        tokens, tokens, both, rows_cols, rows_cols, rows_cols, rows_cols,
        taps, taps, taps, P("row"), cols_rows, both, rows_cols, rows_cols, cols_rows,
    )
    body = partial(local, mesh.shape["col"], mesh.shape["row"])
    return jax.shard_map(body, mesh=mesh, in_specs=in_specs, out_specs=out_specs, check_vma=False)
```

```python
from functools import partial

import jax
import jax.numpy as jnp
from jax import lax
from jax.experimental import pallas as pl
from jax.experimental.pallas import tpu as pltpu
from jax.sharding import PartitionSpec as P

SEQ = 2048
CHUNK = 128
FWD_SUB = 4
BWD_SUB = 2
TILE = 512
HALO = 8
EPSILON = 1e-06
HEAD_FLOOR = 0.002
BF = jnp.bfloat16
F32 = jnp.float32
FFN_TILE = 256
PER_MICRO = 4.0e8


def dot_nn(a, b):
    return lax.dot_general(a, b, (((1,), (0,)), ((), ())), preferred_element_type=F32)


def dot_nt(a, b):
    return lax.dot_general(a, b, (((1,), (1,)), ((), ())), preferred_element_type=F32)


def dot_tn(a, b):
    return lax.dot_general(a, b, (((0,), (0,)), ((), ())), preferred_element_type=F32)


def token_marks(labels, chunk):
    seqs, length = labels.shape
    padded_back = jnp.pad(labels, ((0, 0), (4, 0)), constant_values=-1)
    padded_fore = jnp.pad(labels, ((0, 0), (0, 4)), constant_values=-2)
    marks = [labels]
    for lag in (1, 2, 3):
        marks.append(padded_back[:, 4 - lag : 4 - lag + length] == labels)
    for lag in (1, 2, 3):
        marks.append(padded_fore[:, lag : lag + length] == labels)
    grid = labels.reshape(seqs, length // chunk, chunk)
    prior = jnp.pad(grid[:, :-1, -1], ((0, 0), (1, 0)), constant_values=-1)
    marks.append((grid == prior[:, :, None]).reshape(seqs, length))
    marks.append((grid == grid[:, :, -1:]).reshape(seqs, length))
    marks.append(
        jnp.broadcast_to((grid[:, :, -1] == prior)[:, :, None], grid.shape).reshape(seqs, length)
    )
    marks += [jnp.zeros_like(labels)] * (16 - len(marks))
    marks = [mark.astype(F32).reshape(seqs, length // chunk, 1, chunk) for mark in marks]
    return jnp.concatenate(marks, axis=2)


LABEL, BACK, FORE, CARRIED, LAST, KEEP = 0, 0, 3, 7, 8, 9


def sigmoid(x):
    return 1.0 / (1.0 + jnp.exp(-x))


def level_marks(size):
    row = lax.broadcasted_iota(jnp.int32, (size, size), 0)
    col = lax.broadcasted_iota(jnp.int32, (size, size), 1)
    return row == col, row ^ col


def unit_lower_inverses(systems):
    size = systems[0].shape[0]
    diagonal, differ = level_marks(size)
    inverses = [
        (jnp.where(diagonal, 1.0, 0.0) - jnp.where(differ == 1, system, 0.0)).astype(BF)
        for system in systems
    ]
    block = 2
    while block < size:
        level = (differ >= block) & (differ < 2 * block)
        offs = [jnp.where(level, system, 0.0).astype(BF) for system in systems]
        lefts = [dot_nn(inverse, off).astype(BF) for inverse, off in zip(inverses, offs)]
        inverses = [
            inverse - dot_nn(left, inverse).astype(BF) for inverse, left in zip(inverses, lefts)
        ]
        block *= 2
    return inverses


def conv_rows(ext, taps, marks, lane, first, chunk):
    here = ext[pl.ds(HALO + first, chunk), lane]
    shifted = [here]
    total = here * taps[0:1, lane]
    for lag in (1, 2, 3):
        moved = ext[pl.ds(HALO + first - lag, chunk), lane] * marks[:, BACK + lag : BACK + lag + 1]
        shifted.append(moved)
        total = total + moved * taps[lag : lag + 1, lane]
    return total, shifted


def chunk_marks(marks_ref, seq, part, chunk):
    by_row = marks_ref[seq, part]
    marks = jnp.transpose(by_row)
    row = lax.broadcasted_iota(jnp.int32, (chunk, chunk), 0)
    col = lax.broadcasted_iota(jnp.int32, (chunk, chunk), 1)
    same = marks[:, LABEL : LABEL + 1] == by_row[LABEL : LABEL + 1, :]
    return (
        marks,
        same & (row > col),
        same & (row >= col),
        marks[:, CARRIED : CARRIED + 1],
        marks[:, LAST : LAST + 1],
        marks[0:1, KEEP : KEEP + 1],
    )


def mix_fwd_kernel(
    heads, chunk, sub, marks_ref, taps_ref, gain_ref, pre_ref,
    ao_ref, o_ref, u_ref, w_ref, state_ref, inv_ref, ext, memory,
):
    seqs = pre_ref.shape[0]
    wide = 3 * heads * 128
    size = sub * chunk

    @pl.when(pl.program_id(0) == 0)
    def _():
        ext[:, 0:HALO, :] = jnp.zeros((seqs, HALO, wide), F32)
        memory[...] = jnp.zeros_like(memory)

    ext[:, HALO : HALO + size, :] = pre_ref[:, :, 0:wide]
    kept = {
        (seq, part): chunk_marks(marks_ref, seq, part, chunk)
        for seq in range(seqs)
        for part in range(sub)
    }
    chains = [(seq, head) for seq in range(seqs) for head in range(heads)]
    units = [(seq, head, part) for part in range(sub) for seq, head in chains]
    boths, values, betas, attns, keys_list, systems = {}, {}, {}, {}, {}, {}
    for unit in units:
        seq, head, part = unit
        marks = kept[seq, part][0]
        acts = []
        for kind in range(3):
            lane = pl.ds((kind * heads + head) * 128, 128)
            cv, _ = conv_rows(ext.at[seq], taps_ref, marks, lane, part * chunk, chunk)
            acts.append(cv * sigmoid(cv))
        q1, k1, values[unit] = acts
        qn = q1 * (lax.rsqrt(jnp.sum(q1 * q1, axis=1, keepdims=True) + EPSILON) * 128 ** (-0.5))
        kn = k1 * lax.rsqrt(jnp.sum(k1 * k1, axis=1, keepdims=True) + EPSILON)
        betas[unit] = sigmoid(
            pre_ref[seq, part * chunk : (part + 1) * chunk, wide + head : wide + head + 1]
        )
        boths[unit] = jnp.concatenate([qn.astype(BF), kn.astype(BF)], axis=0)
    for unit in units:
        _, strict, within, _, _, _ = kept[unit[0], unit[2]]
        scores = dot_nt(boths[unit], boths[unit][chunk:])
        attns[unit] = jnp.where(within, scores[:chunk], 0.0).astype(BF)
        keys = jnp.where(strict, scores[chunk:], 0.0)
        keys_list[unit] = keys.astype(BF)
        systems[unit] = keys * betas[unit]
    inverses = dict(zip(units, unit_lower_inverses([systems[unit] for unit in units])))
    for part in range(sub):
        here = [(seq, head, part) for seq, head in chains]
        states = [memory[index] for index in range(len(here))]
        lows = [state.astype(BF) for state in states]
        seens = [dot_nn(boths[unit], low) for unit, low in zip(here, lows)]
        rights = [
            values[unit] - kept[unit[0], part][3] * seen[chunk:]
            for unit, seen in zip(here, seens)
        ]
        updates = [
            dot_nn(inverses[unit], (betas[unit] * right).astype(BF))
            for unit, right in zip(here, rights)
        ]
        for index, unit in enumerate(here):
            last, keep = kept[unit[0], part][4:]
            memory[index] = keep * states[index] + dot_tn(
                boths[unit][chunk:], (last * updates[index]).astype(BF)
            )
        for index, unit in enumerate(here):
            seq, head, _ = unit
            carried = kept[seq, part][3]
            rows = slice(part * chunk, (part + 1) * chunk)
            ub = updates[index].astype(BF)
            mixed = dot_nn(jnp.concatenate([attns[unit], keys_list[unit]], axis=0), ub)
            out = carried * seens[index][:chunk] + mixed[:chunk]
            wrong = rights[index] - mixed[chunk:]
            lane = pl.ds(head * 128, 128)
            scale = lax.rsqrt(jnp.maximum(jnp.mean(out * out, axis=1, keepdims=True), HEAD_FLOOR))
            ao_ref[seq, rows, lane] = (out * scale * gain_ref[...]).astype(BF)
            o_ref[seq, rows, lane] = out
            u_ref[seq, rows, lane] = ub
            w_ref[seq, rows, lane] = wrong.astype(BF)
            inv_ref[part, index] = inverses[unit]
            state_ref[part, index] = lows[index]
    ext[:, 0:HALO, :] = ext[:, size : size + HALO, :]


def mix_bwd_kernel(
    heads, chunk, sub, marks_ref, taps_ref, gain_ref,
    o_ref, u_ref, w_ref, state_ref, inv_ref, pre_ref, halo_ref, dao_ref,
    dpre_ref, stat_ref, dconv_ref, dgain_ref, ext, dext, memory,
):
    seqs = pre_ref.shape[0]
    wide = 3 * heads * 128
    size = sub * chunk

    @pl.when(pl.program_id(0) == 0)
    def _():
        dext[:, size : size + HALO, :] = jnp.zeros((seqs, HALO, wide), F32)
        memory[...] = jnp.zeros_like(memory)
        dconv_ref[...] = jnp.zeros_like(dconv_ref)
        dgain_ref[...] = jnp.zeros_like(dgain_ref)

    ext[:, 0:HALO, :] = halo_ref[:, :, 0:wide]
    ext[:, HALO : HALO + size, :] = pre_ref[:, :, 0:wide]
    gain = gain_ref[...]

    def fold(rows):
        return jnp.sum(rows.reshape(chunk // 8, 8, 128), axis=0)

    kept = {
        (seq, part): chunk_marks(marks_ref, seq, part, chunk)
        for seq in range(seqs)
        for part in range(sub)
    }
    chains = [(seq, head) for seq in range(seqs) for head in range(heads)]
    units = [(seq, head, part) for part in reversed(range(sub)) for seq, head in chains]

    def rows_of(unit):
        return slice(unit[2] * chunk, (unit[2] + 1) * chunk)

    def lane_of(unit, kind=0):
        return pl.ds((kind * heads + unit[1]) * 128, 128)

    acts, scales, norms, betas, boths, dobs, cdos = {}, {}, {}, {}, {}, {}, {}
    for unit in units:
        seq, head, part = unit
        marks, _, _, carried, _, _ = kept[seq, part]
        for kind in range(3):
            cv, _ = conv_rows(
                ext.at[seq], taps_ref, marks, lane_of(unit, kind), part * chunk, chunk
            )
            sg = sigmoid(cv)
            acts[unit, kind] = cv * sg
            scales[unit, kind] = sg * (1.0 + cv * (1.0 - sg))
        q1, k1 = acts[unit, 0], acts[unit, 1]
        rq = lax.rsqrt(jnp.sum(q1 * q1, axis=1, keepdims=True) + EPSILON)
        rk = lax.rsqrt(jnp.sum(k1 * k1, axis=1, keepdims=True) + EPSILON)
        norms[unit] = rq, rk
        boths[unit] = jnp.concatenate(
            [(q1 * (rq * 128 ** (-0.5))).astype(BF), (k1 * rk).astype(BF)], axis=0
        )
        betas[unit] = sigmoid(pre_ref[seq, rows_of(unit), wide + head : wide + head + 1])
        out = o_ref[seq, rows_of(unit), lane_of(unit)]
        square = jnp.mean(out * out, axis=1, keepdims=True)
        scale = lax.rsqrt(jnp.maximum(square, HEAD_FLOOR))
        ro = out * scale
        dao = dao_ref[seq, rows_of(unit), lane_of(unit)]
        dgain_ref[...] += fold(dao * ro)
        eo = dao * gain
        inner = jnp.mean(eo * ro, axis=1, keepdims=True)
        inner = jnp.where(square > HEAD_FLOOR, inner, 0.0)
        do = scale * (eo - ro * inner)
        dobs[unit] = do.astype(BF)
        cdos[unit] = (carried * do).astype(BF)
    firsts, grows, crosses = {}, {}, {}
    for unit in units:
        _, _, within, _, _, _ = kept[unit[0], unit[2]]
        both = boths[unit]
        attn = jnp.where(within, dot_nt(both[:chunk], both[chunk:]), 0.0).astype(BF)
        firsts[unit] = dot_tn(attn, dobs[unit])
        grows[unit] = dot_tn(both[:chunk], cdos[unit])
    drs, seconds, dbetas = {}, {}, {}
    for part in reversed(range(sub)):
        here = [(seq, head, part) for seq, head in chains]
        olds = [memory[index] for index in range(len(here))]
        lows = [old.astype(BF) for old in olds]
        fromstate = [dot_nn(boths[unit][chunk:], low) for unit, low in zip(here, lows)]
        dus = [
            (firsts[unit] + kept[unit[0], part][4] * term).astype(BF)
            for unit, term in zip(here, fromstate)
        ]
        drhs = [dot_tn(inv_ref[part, index], du) for index, du in enumerate(dus)]
        for index, unit in enumerate(here):
            drs[unit] = betas[unit] * drhs[index]
            carried, _, keep = kept[unit[0], part][3:]
            memory[index] = (
                keep * olds[index]
                + grows[unit]
                - dot_tn(boths[unit][chunk:], (carried * drs[unit]).astype(BF))
            )
        for index, unit in enumerate(here):
            wrong = w_ref[unit[0], rows_of(unit), lane_of(unit)].astype(F32)
            dbetas[unit] = jnp.sum(drhs[index] * wrong, axis=1, keepdims=True)
            seconds[unit] = dot_nt(u_ref[unit[0], rows_of(unit), lane_of(unit)], lows[index])
    shares = {}
    for unit in units:
        seq, head, part = unit
        marks, strict, within, carried, last, _ = kept[seq, part]
        both, kb = boths[unit], boths[unit][chunk:]
        index = seq * heads + head
        stack = jnp.concatenate([dobs[unit], drs[unit].astype(BF)], axis=0)
        right = jnp.concatenate(
            [u_ref[seq, rows_of(unit), lane_of(unit)], state_ref[part, index]], axis=0
        )
        cross = dot_nt(stack, right)
        dattn = jnp.where(within, cross[:chunk, :chunk], 0.0).astype(BF)
        dkeys = jnp.where(strict, -cross[chunk:, :chunk], 0.0).astype(BF)
        dboth = jnp.concatenate([dattn, dkeys], axis=0)
        by_row = dot_nn(dboth, kb)
        dqn = carried * cross[:chunk, chunk:] + by_row[:chunk]
        dkn = (
            dot_tn(dboth, both)
            + last * seconds[unit]
            + by_row[chunk:]
            - carried * cross[chunk:, chunk:]
        )
        (rq, rk), q1, k1 = norms[unit], acts[unit, 0], acts[unit, 1]
        dq1 = 128 ** (-0.5) * rq * (
            dqn - (rq * rq) * q1 * jnp.sum(q1 * dqn, axis=1, keepdims=True)
        )
        dk1 = rk * (dkn - (rk * rk) * k1 * jnp.sum(k1 * dkn, axis=1, keepdims=True))
        for kind, dact in enumerate((dq1, dk1, drs[unit])):
            dext[seq, rows_of(unit), lane_of(unit, kind)] = dact * scales[unit, kind]
    for unit in units:
        seq, head, part = unit
        marks = kept[seq, part][0]
        share = shares.get((seq, part), 0.0)
        for kind in range(3):
            lane = lane_of(unit, kind)
            _, shifts = conv_rows(ext.at[seq], taps_ref, marks, lane, part * chunk, chunk)
            dc = dext[seq, rows_of(unit), lane]
            back = dc * taps_ref[0:1, lane]
            dconv_ref[0:8, lane] += fold(dc * shifts[0])
            for lag in (1, 2, 3):
                dconv_ref[8 * lag : 8 * lag + 8, lane] += fold(dc * shifts[lag])
                back = back + (
                    dext[seq, pl.ds(part * chunk + lag, chunk), lane]
                    * marks[:, FORE + lag : FORE + lag + 1]
                    * taps_ref[lag : lag + 1, lane]
                )
            dpre_ref[seq, rows_of(unit), lane] = back.astype(BF)
            share = share + back * shifts[0]
        shares[seq, part] = share
    column = lax.broadcasted_iota(jnp.int32, (chunk, 128), 1)
    for seq, part in kept:
        rows = slice(part * chunk, (part + 1) * chunk)
        total = jnp.zeros((chunk, 128), F32)
        for head in range(heads):
            unit = seq, head, part
            grad = dbetas[unit] * betas[unit] * (1.0 - betas[unit])
            total = jnp.where(column == head, grad, total)
        dpre_ref[seq, rows, pl.ds(wide, 128)] = total.astype(BF)
        share = shares[seq, part] + total * pre_ref[seq, rows, pl.ds(wide, 128)]
        stat_ref[seq, rows] = jnp.broadcast_to(
            jnp.sum(share, axis=1, keepdims=True), (chunk, 128)
        )
    dext[:, size : size + HALO, :] = dext[:, 0:HALO, :]


def params():
    return pltpu.CompilerParams(dimension_semantics=("arbitrary",), vmem_limit_bytes=60 * 2**20)


def fixed(array):
    zeros = (0,) * array.ndim
    return pl.BlockSpec(array.shape, lambda n: zeros, pipeline_mode=pl.Buffered(1))


def cost(micros):
    return pl.CostEstimate(flops=int(micros * PER_MICRO), bytes_accessed=0, transcendentals=0)


def shape(dims, dtype):
    return jax.ShapeDtypeStruct(dims, dtype)


def mix_forward(pre, marks, taps, gain, heads, chunk=CHUNK, sub=FWD_SUB):
    seqs, length, cols = pre.shape
    chains, parts = seqs * heads, length // chunk
    steps = parts // sub
    wide, hw = 3 * heads * 128, heads * 128

    def tok(width):
        return pl.BlockSpec((seqs, sub * chunk, width), lambda n: (0, n, 0))

    out_shape = [
        shape((seqs, length, hw), BF),
        shape((seqs, length, hw), F32),
        shape((seqs, length, hw), BF),
        shape((seqs, length, hw), BF),
        shape((parts, chains, 128, 128), BF),
        shape((parts, chains, chunk, chunk), BF),
    ]
    mixed, *saved = pl.pallas_call(
        partial(mix_fwd_kernel, heads, chunk, sub),
        grid=(steps,),
        in_specs=[
            pl.BlockSpec((seqs, sub, 16, chunk), lambda n: (0, n, 0, 0)),
            fixed(taps), fixed(gain), tok(cols),
        ],
        out_specs=[tok(hw)] * 4 + [
            pl.BlockSpec((sub, chains, 128, 128), lambda n: (n, 0, 0, 0)),
            pl.BlockSpec((sub, chains, chunk, chunk), lambda n: (n, 0, 0, 0)),
        ],
        out_shape=out_shape,
        scratch_shapes=[
            pltpu.VMEM((seqs, HALO + sub * chunk, wide), F32),
            pltpu.VMEM((chains, 128, 128), F32),
        ],
        compiler_params=params(),
        cost_estimate=cost(24),
        name="mix_forward",
    )(marks, taps, gain, pre)
    return mixed, saved


def mix_backward(pre, marks, taps, gain, saved, dao, heads, chunk=CHUNK, sub=BWD_SUB):
    seqs, length, cols = pre.shape
    chains, parts = seqs * heads, length // chunk
    steps = parts // sub
    wide, hw = 3 * heads * 128, heads * 128
    end, groups = steps - 1, sub * chunk // HALO

    def tok(width):
        return pl.BlockSpec((seqs, sub * chunk, width), lambda n: (0, end - n, 0))

    halo = pl.BlockSpec(
        (seqs, HALO, cols), lambda n: (0, jnp.maximum((end - n) * groups - 1, 0), 0)
    )
    out_shape = [
        shape((seqs, length, cols), BF), shape((seqs, length, 128), F32),
        shape((32, wide), F32), shape((8, 128), F32),
    ]
    return pl.pallas_call(
        partial(mix_bwd_kernel, heads, chunk, sub),
        grid=(steps,),
        in_specs=[
            pl.BlockSpec((seqs, sub, 16, chunk), lambda n: (0, end - n, 0, 0)),
            fixed(taps), fixed(gain),
        ] + [tok(hw)] * 3 + [
            pl.BlockSpec((sub, chains, 128, 128), lambda n: (end - n, 0, 0, 0)),
            pl.BlockSpec((sub, chains, chunk, chunk), lambda n: (end - n, 0, 0, 0)),
            tok(cols), halo, tok(hw),
        ],
        out_specs=[
            tok(cols), tok(128),
            pl.BlockSpec((32, wide), lambda n: (0, 0)),
            pl.BlockSpec((8, 128), lambda n: (0, 0)),
        ],
        out_shape=out_shape,
        scratch_shapes=[
            pltpu.VMEM((seqs, HALO + sub * chunk, wide), F32),
            pltpu.VMEM((seqs, HALO + sub * chunk, wide), F32),
            pltpu.VMEM((chains, 128, 128), F32),
        ],
        compiler_params=params(),
        cost_estimate=cost(34),
        name="mix_backward",
    )(marks, taps, gain, *saved, pre, pre, dao)


def swap(values, bit, ways):
    return lax.ppermute(values, "col", [(i, i ^ bit) for i in range(ways)])


def gather_near(values, ways):
    base = [(0, 0, values)]
    if ways == 8:
        return base + [(far, 0, swap(values, far, ways)) for far in (2, 4)]
    bit = 2
    while bit < ways:
        base += [(far ^ bit, lane, swap(array, bit, ways)) for far, lane, array in base]
        bit *= 2
    return base


def gather_far(base, ways, *others):
    if ways != 8:
        return base
    along, across = base[1][2], base[2][2]
    half = along.shape[-1] // 2
    first, second = across[..., :half], along[..., half:]
    if others:
        first, second = after((first, second), others)
    return base + [(6, 0, swap(first, 2, ways)), (6, half, swap(second, 4, ways))]


def gather_cols(values, ways, way="direct"):
    base = gather_near(values, ways)
    if ways != 8 or way == "split":
        return gather_far(base, ways)
    return base + [(6, 0, swap(values, 6, ways))]


def other_core(base, ways):
    return base + [(far ^ 1, lane, swap(array, 1, ways)) for far, lane, array in base]


def after(values, *others):
    return lax.optimization_barrier((values, others))[0]


def arrays_of(pieces):
    return [array for _, _, array in pieces]


def pieces_after(pieces, *others):
    arrays = after(arrays_of(pieces), *others)
    return [(far, lane, array) for (far, lane, _), array in zip(pieces, arrays)]


def covered(results, pieces):
    results, arrays = lax.optimization_barrier((results, arrays_of(pieces)))
    return results, [(far, lane, array) for (far, lane, _), array in zip(pieces, arrays)]


def add_low(*terms):
    return sum(term.astype(F32) for term in terms).astype(BF)


def send_pairs(pieces, ways):
    return [(far, 0, swap(pieces[far | 1], 1, ways)) for far in range(0, ways, 2)]


def add_pairs(pieces, arrived):
    sums = [(far, 0, add_low(pieces[far], array)) for far, _, array in arrived if far]
    return (pieces[0], arrived[0][2]), sums


def scatter_cols(sums, ways, way="direct"):
    held = {far: array for far, _, array in sums}
    if ways == 8 and way == "direct":
        return [(far, 0, swap(held[far], far, ways)) for far in (2, 4, 6)]
    if ways == 8:
        half = held[2].shape[-1] // 2
        left = swap(held[6][..., :half], 2, ways)
        right = swap(held[6][..., half:], 4, ways)
        four = jnp.concatenate(
            [add_low(left, held[4][..., :half]), held[4][..., half:]], axis=-1
        )
        two = jnp.concatenate(
            [held[2][..., :half], add_low(right, held[2][..., half:])], axis=-1
        )
        return [(2, 0, swap(two, 2, ways)), (4, 0, swap(four, 4, ways))]
    terms = {far: (array,) for far, array in held.items()}
    terms[0] = ()
    bit = 2
    while bit < ways:
        terms = {
            far: terms[far] + (swap(add_low(*terms[far | bit]), bit, ways),)
            for far in terms
            if not far & bit
        }
        bit *= 2
    return [(0, 0, array) for array in terms[0]]


def total_of(own, arrived):
    return sum(array.astype(F32) for array in (*own, *arrays_of(arrived)))


def sum_over(values, axis, ways, bit=1, size=None):
    size = ways if size is None else size
    while bit < ways:
        values = values + lax.ppermute(values, axis, [(i, i ^ bit) for i in range(size)])
        bit *= 2
    return values


def sum_cols(values, ways):
    values = values + swap(values, 1, ways)
    return values + sum(swap(values, far, ways) for far in range(2, ways, 2))


def whole_blocks(layout, pieces):
    blocks = {}
    for (far, _), piece in zip(layout, pieces):
        blocks.setdefault(far, []).append(piece[...])
    return {
        far: parts[0] if len(parts) == 1 else jnp.concatenate(parts, axis=1)
        for far, parts in blocks.items()
    }


def lanes_of(spot_ref, far, block):
    return pl.ds(pl.multiple_of((spot_ref[0] ^ far) * block, block), block)


def part_of(spot_ref, far, block, step):
    index, each = spot_ref[0] ^ far, step // block
    return index // each, pl.ds(pl.multiple_of((index % each) * block, block), block)


def normed(blocks, spot_ref, gain_ref, act_ref, block):
    width = act_ref.shape[1]
    total = 0.0
    for rows in blocks.values():
        rows = rows.astype(F32)
        total = total + jnp.sum(rows * rows, axis=1, keepdims=True)
    inverse = lax.rsqrt(total / width + EPSILON)
    acts = {}
    for far, rows in blocks.items():
        lanes = lanes_of(spot_ref, far, block)
        acts[far] = (rows.astype(F32) * inverse * gain_ref[0:1, lanes]).astype(BF)
        act_ref[:, lanes] = acts[far]
    return acts, inverse


def project_kernel(layout, block, spot_ref, gain_ref, weight_ref, *refs):
    pieces, (pre_ref, act_ref, stat_ref) = refs[: len(layout)], refs[len(layout) :]
    blocks = whole_blocks(layout, pieces)
    acts, inverse = normed(blocks, spot_ref, gain_ref, act_ref, block)
    stat_ref[...] = jnp.broadcast_to(inverse, stat_ref.shape)
    total = 0.0
    for far, act in acts.items():
        total = total + dot_nn(act, weight_ref[lanes_of(spot_ref, far, block), :])
    pre_ref[...] = total


def spread_kernel(transposed, block, spot_ref, weight_ref, rows_ref, *outs):
    rows = rows_ref[...]
    step = weight_ref.shape[1 if transposed else 2]
    for far, out in enumerate(outs):
        part, lanes = part_of(spot_ref, far, block, step)
        if transposed:
            out[...] = dot_nt(rows, weight_ref[part, lanes, :]).astype(BF)
        else:
            out[...] = dot_nn(rows, weight_ref[part, :, lanes]).astype(BF)


def collect_kernel(layout, block, spot_ref, weight_ref, *refs):
    pieces, (whole_ref, out_ref) = refs[: len(layout)], refs[len(layout) :]
    for far, rows in whole_blocks(layout, pieces).items():
        whole_ref[:, lanes_of(spot_ref, far, block)] = rows
    step = weight_ref.shape[2]
    total = 0.0
    for part in range(weight_ref.shape[0]):
        total = total + dot_nt(
            whole_ref[:, part * step : (part + 1) * step], weight_ref[part]
        )
    out_ref[...] = total


def ffn_kernel(layout, cot_layout, block, ways, spot_ref, gain_ref, gates_ref, ups_ref, down_ref, *refs):
    count, total = len(layout), len(layout) + len(cot_layout)
    acts, cots, refs = refs[:count], refs[count:total], refs[total:]
    act_ref, cot_ref, hid_ref, dgate_ref, dup_ref, stat_ref = refs[:6]
    grads, outs = refs[6 : 6 + ways], refs[6 + ways : -4]
    whole, gates, ups, downs = refs[-4:]

    @pl.when(pl.program_id(0) == 0)
    def _():
        step = down_ref.shape[2]
        for part in range(down_ref.shape[0]):
            lanes = slice(part * step, (part + 1) * step)
            gates[:, lanes] = gates_ref[part]
            ups[:, lanes] = ups_ref[part]
            downs[:, lanes] = down_ref[part]

    for far, rows in whole_blocks(cot_layout, cots).items():
        cot_ref[:, lanes_of(spot_ref, far, block)] = rows
    _, inverse = normed(whole_blocks(layout, acts), spot_ref, gain_ref, act_ref, block)
    dhid = dot_nt(cot_ref[...], downs[...])
    gate = dot_nt(act_ref[...], gates[...])
    up = dot_nt(act_ref[...], ups[...])
    sig = sigmoid(gate)
    swish = gate * sig
    hid = (swish * up).astype(BF)
    dgate = (dhid * up * sig * (1.0 + gate * (1.0 - sig))).astype(BF)
    dup = (dhid * swish).astype(BF)
    hid_ref[...] = hid
    dgate_ref[...] = dgate
    dup_ref[...] = dup
    inner = jnp.sum(dgate.astype(F32) * gate + dup.astype(F32) * up, axis=1, keepdims=True)
    lane = lax.broadcasted_iota(jnp.int32, stat_ref.shape, 1)
    stat_ref[...] = jnp.where(lane == 0, inverse, inner)
    whole[...] = (dot_nn(dgate, gates[...]) + dot_nn(dup, ups[...])).astype(BF)
    for far, grad in enumerate(grads):
        grad[...] = whole[:, lanes_of(spot_ref, far, block)]
    if len(outs) == 1:
        outs[0][...] = dot_nn(hid, downs[...]).astype(BF)
    else:
        whole[...] = dot_nn(hid, downs[...]).astype(BF)
        for far, out in enumerate(outs):
            out[...] = whole[:, lanes_of(spot_ref, far, block)]


SPOT = pl.BlockSpec(memory_space=pltpu.SMEM)


def rows_spec(width, tile):
    return pl.BlockSpec((tile, width), lambda n: (n, 0))


def tiled(kernel, name, fixed_args, row_args, out_shape, tile, micros, spot, scratch=()):
    rows = row_args[0].shape[0]
    return pl.pallas_call(
        kernel,
        grid=(rows // tile,),
        in_specs=[SPOT]
        + [fixed(a) for a in fixed_args]
        + [rows_spec(a.shape[1], tile) for a in row_args],
        out_specs=[rows_spec(a.shape[1], tile) for a in out_shape],
        out_shape=out_shape,
        scratch_shapes=list(scratch),
        compiler_params=params(),
        cost_estimate=cost(micros),
        name=name,
    )(spot, *fixed_args, *row_args)


def layout_of(pieces):
    return tuple((far, lane) for far, lane, _ in pieces), [array for _, _, array in pieces]


def project(pieces, gain, weight, spot, block):
    layout, arrays = layout_of(pieces)
    rows, (width, cols) = arrays[0].shape[0], weight.shape
    out = [shape((rows, cols), F32), shape((rows, width), BF), shape((rows, 128), F32)]
    return tiled(
        partial(project_kernel, layout, block), "project", [gain, weight], arrays, out,
        TILE, 19, spot,
    )


def spread(rows_in, weight, spot, block, ways, transposed):
    rows = rows_in.shape[0]
    return tiled(
        partial(spread_kernel, transposed, block), "spread", [weight], [rows_in],
        [shape((rows, block), BF)] * ways, TILE, 14 if transposed else 7, spot,
    )


def collect(pieces, weight, spot, block, ways):
    layout, arrays = layout_of(pieces)
    rows = arrays[0].shape[0]
    out = [shape((rows, block * ways), BF), shape((rows, weight.shape[1]), F32)]
    return tiled(
        partial(collect_kernel, layout, block), "collect", [weight], arrays, out,
        TILE, 9, spot,
    )


def feed_forward(acts, cots, gain, gates, ups, down, spot, block, ways, split):
    layout, act_arrays = layout_of(acts)
    cot_layout, cot_arrays = layout_of(cots)
    rows, width, hidden = act_arrays[0].shape[0], block * ways, down.shape[1]
    out = (
        [shape((rows, width), BF)] * 2
        + [shape((rows, hidden), BF)] * 3
        + [shape((rows, 128), F32)]
        + [shape((rows, block), BF)] * ways
        + ([shape((rows, block), BF)] * ways if split else [shape((rows, width), BF)])
    )
    results = tiled(
        partial(ffn_kernel, layout, cot_layout, block, ways), "feed_forward", [gain, gates, ups, down],
        act_arrays + cot_arrays, out, FFN_TILE, 54, spot,
        [pltpu.VMEM((FFN_TILE, width), BF)] + [pltpu.VMEM((hidden, width), BF)] * 3,
    )
    return results[:6], results[6 : 6 + ways], results[6 + ways :]


def outer(lefts, rights):
    total = None
    for left, right in zip(lefts, rights):
        term = dot_tn(left, right)
        total = term if total is None else total + term
    return total


def grow(total, left, right, last):
    term = dot_tn(left, right)
    term = term if total is None else total + term
    return term.astype(BF) if last else term


def scatter_row(values, dim):
    return lax.psum_scatter(
        values.astype(BF), "row", scatter_dimension=dim, tiled=True
    )


def local(
    ways, rows_ways, inputs, cotangent, segment, norm_gain, w_query, w_key, w_value, w_beta,
    conv_query, conv_key, conv_value, head_gain, w_out, ffn_gain, w_gate, w_up, w_down,
):
    micro, tokens, block = inputs.shape
    width = block * ways
    heads = w_beta.shape[1]
    hw = heads * 128
    per = tokens // SEQ
    here = lax.axis_index("col")
    spot = here.astype(jnp.int32)[None]

    share, taps_share = norm_gain.shape[0], conv_query.size
    packed = jnp.concatenate(
        [norm_gain, ffn_gain]
        + [taps.reshape(-1) for taps in (conv_query, conv_key, conv_value)]
        + [head_gain]
    )
    row = lax.axis_index("row")
    packed = lax.dynamic_update_slice(
        jnp.zeros((ways * rows_ways, packed.shape[0]), BF), packed[None], (here * rows_ways + row, 0)
    )
    packed = sum_over(packed, "col", ways, 2)
    first_share = after(inputs[0], packed)
    packed = sum_over(sum_over(packed, "col", 2, 1, ways), "row", rows_ways)
    gain_one = packed[:, :share].reshape(1, width).astype(F32)
    gain_two = packed[:, share : 2 * share].reshape(1, width).astype(F32)
    mine = lax.dynamic_slice_in_dim(packed, here * rows_ways, rows_ways, axis=0).astype(F32)
    taps = mine[:, 2 * share : 2 * share + 3 * taps_share]
    taps = taps.reshape(rows_ways, 3, share, 4).transpose(3, 1, 0, 2).reshape(4, 3 * hw)
    taps = jnp.pad(taps, ((0, 4), (0, 0)))
    gain_head = mine[:, 2 * share + 3 * taps_share :].reshape(1, 128)
    own_one = lax.dynamic_slice_in_dim(gain_one, here * block, block, axis=1)
    own_two = lax.dynamic_slice_in_dim(gain_two, here * block, block, axis=1)

    beta_wide = jnp.pad(w_beta, ((0, 0), (0, 128 - heads)))
    qkv_share = jnp.concatenate([w_query, w_key, w_value, beta_wide], axis=1)
    qkv = lax.all_gather(qkv_share, "row", axis=0, tiled=False)
    out_parts = lax.all_gather(w_out, "row", axis=0, tiled=False)
    gates = lax.all_gather(w_gate.T, "row", axis=0, tiled=False)
    ups = lax.all_gather(w_up.T, "row", axis=0, tiled=False)
    down = lax.all_gather(w_down, "row", axis=0, tiled=False)

    data = [token_marks(segment[m].reshape(per, SEQ), CHUNK) for m in range(micro)]
    x_base, cot_near, mine = [], [], first_share
    for m in range(micro):
        near = gather_near(mine, ways)
        x_base.append(gather_far(near, ways))
        if m < micro - 1:
            mine = after(inputs[m + 1], arrays_of(near))
    for m in range(micro):
        mine = after(cotangent[m], arrays_of(x_base[-1]))
        cot_near.append(gather_near(mine, ways))
    cot_base = []
    weight = qkv.reshape(width, -1)
    pres, act_ones, inv_ones, mixed, saved = [], [], [], [], []
    resids, act_base = [], []

    def add_residual(m, own, arrived):
        resids.append(inputs[m].astype(F32) + total_of(own, arrived))
        if m:
            act_base.append(gather_cols(resids[m].astype(BF), ways))
            return
        near = gather_near(resids[m].astype(BF), ways)
        act_base.append(gather_far(near, ways))

    flying = None
    for m in range(micro):
        pieces = other_core(x_base[m], ways)
        if m:
            own, pairs = add_pairs(sums, send_pairs(sums, ways))
            flying = own, scatter_cols(pairs, ways)
            pieces = pieces_after(pieces, arrays_of(pairs))
        pre, act, stat = project(pieces, gain_one, weight, spot, block)
        if m:
            pre, cot_base[m - 1] = covered(pre, cot_base[m - 1])
            if m == micro - 1:
                pre, gates = lax.optimization_barrier((pre, gates))
        pres.append(pre.reshape(per, SEQ, -1))
        act_ones.append(act)
        inv_ones.append(stat[:, 0:1])
        array, rest = mix_forward(pres[m], data[m], taps, gain_head, heads)
        if m < micro - 1:
            cot_base.append(gather_far(cot_near[m], ways, array))
            array, x_base[m + 1] = covered(array, x_base[m + 1])
        else:
            array, cot_base[m] = covered(array, cot_base[m])
        mixed.append(array.reshape(tokens, hw))
        saved.append(rest)
        sums = spread(mixed[m], out_parts, spot, block, ways, False)
        if m == micro - 2:
            cot_base.append(gather_far(cot_near[m + 1], ways, sums))
        if flying:
            sums, arrived = covered(sums, flying[1])
            add_residual(m - 1, flying[0], arrived)
            sums = after(sums, resids[m - 1])
        if m == micro - 1:
            sums, ups = lax.optimization_barrier((sums, ups))
    own, pairs = add_pairs(sums, send_pairs(sums, ways))
    arrived = scatter_cols(pairs, ways, "split")
    add_residual(micro - 1, own, arrived)
    cots = [other_core(base, ways) for base in cot_base]

    ffn_saved, ffn_outs, inners, resid_grads, grad_base = [], [], [], [], []
    down_grad, gate_grad, up_grad, gain_two_grad = None, None, None, 0.0

    def finish_ffn(m, own, arrived):
        inverse = ffn_saved[m][5][:, 0:1]
        act_grad = total_of(own, arrived)
        unit = resids[m] * inverse
        resid_grads.append(
            cotangent[m].astype(F32) + inverse * (act_grad * own_two - unit * inners[m])
        )
        grad_base.append(gather_near(resid_grads[m].astype(BF), ways))
        return jnp.sum(act_grad * unit, axis=0)

    flying = None
    for m in range(micro):
        last = m == micro - 1
        pieces = other_core(act_base[m], ways)
        pieces = pieces_after(pieces, resids, down_grad, arrays_of(pairs))
        kept, grads, outs = feed_forward(
            pieces, cots[m], gain_two, gates, ups, down, spot, block, ways, last
        )
        if not last:
            (kept, grads, outs), act_base[m + 1] = covered(
                (kept, grads, outs), act_base[m + 1]
            )
        if flying:
            before = ffn_saved[m - 1]
            left = after(before[0], kept[5])
            gate_grad = grow(gate_grad, before[3], left, False)
            up_grad = grow(up_grad, before[4], after(left, gate_grad), False)
            (kept, grads, outs, gate_grad, up_grad), arrived = covered(
                (kept, grads, outs, gate_grad, up_grad), flying[1]
            )
            gain_two_grad = gain_two_grad + finish_ffn(m - 1, flying[0], arrived)
            kept, grads, ffn_outs[m - 1] = lax.optimization_barrier(
                (kept, after(grads, resid_grads[m - 1]), ffn_outs[m - 1])
            )
        ffn_saved.append(kept)
        inners.append(sum_cols(kept[5][:, 1], ways)[:, None] / width)
        down_grad, arrived = covered(
            grow(down_grad, kept[2], kept[1], last), send_pairs(grads, ways)
        )
        own, pairs = add_pairs(grads, arrived)
        if not last:
            flying = own, scatter_cols(pairs, ways)
            ffn_outs.append(
                lax.psum_scatter(outs[0], "col", scatter_dimension=1, tiled=True)
            )
    kept = ffn_saved[-1]
    gate_grad = grow(gate_grad, kept[3], after(kept[0], arrays_of(pairs)), True)
    gate_grad, arrived = covered(gate_grad, send_pairs(outs, ways))
    gate_grad, base = covered(gate_grad, grad_base[0])
    out_own, out_sums = add_pairs(outs, arrived)
    base = gather_far(base, ways)
    right = after(kept[0], gate_grad, arrays_of(out_sums))
    up_grad, base = covered(grow(up_grad, kept[4], right, True), base)
    flying = own, scatter_cols(pieces_after(pairs, arrays_of(base)), ways)
    pieces = other_core(base, ways)
    grad_down = scatter_row(down_grad, 1)
    grad_gate = scatter_row(gate_grad, 1)
    grad_up = scatter_row(up_grad, 1)

    qkv_terms, out_terms, firsts, dconv, dgain = [], [], [], 0.0, 0.0
    behind, means = None, []
    for m in range(micro):
        whole, dao = collect(pieces, out_parts, spot, block, ways)
        if m == micro - 1:
            out_terms.append(dot_tn(mixed[m], whole))
            out_flying = scatter_cols(pieces_after(out_sums, arrays_of(pieces)), ways)
            grad_out = scatter_row(sum(out_terms), 1)
            dao = after(dao, out_terms)
        dpre, stat, dconv_part, dgain_part = mix_backward(
            pres[m], data[m], taps, gain_head, saved[m], dao.reshape(per, SEQ, hw), heads
        )
        dpre = dpre.reshape(tokens, -1)
        dconv, dgain = dconv + dconv_part, dgain + dgain_part
        if m == 0:
            dpre, grad_down = lax.optimization_barrier((dpre, grad_down))
        if flying:
            dpre, arrived = covered(dpre, flying[1])
            gain_two_grad = gain_two_grad + finish_ffn(micro - 1, flying[0], arrived)
            dpre, flying = after(dpre, resid_grads[-1]), None
        if behind:
            dpre, arrived = covered(dpre, behind[1])
            firsts.append((behind[0], arrived))
        if m < micro - 1:
            sums = spread(dpre, qkv, spot, block, ways, True)
            term, arrived = covered(
                dot_tn(act_ones[m], after(dpre, sums)), send_pairs(sums, ways)
            )
            means.append(sum_cols(stat.reshape(tokens, 128)[:, 0], ways)[:, None] / width)
            own, pairs = add_pairs(sums, arrived)
            term, base = covered(term, grad_base[m + 1])
            base = gather_far(base, ways)
            qkv_terms.append(term)
            out_term = dot_tn(mixed[m], after(whole, term, arrays_of(pairs)))
            out_term, base = covered(out_term, base)
            behind = own, scatter_cols(pieces_after(pairs, arrays_of(base)), ways)
            out_terms.append(out_term)
            pieces = pieces_after(other_core(base, ways), out_term)
        else:
            dpre, grad_gate, grad_up, grad_out, means = lax.optimization_barrier(
                (dpre, grad_gate, grad_up, grad_out, means)
            )
            qkv_grad = (sum(qkv_terms) + dot_tn(act_ones[m], dpre)).astype(BF)
            dpre = after(dpre, qkv_grad)
            grad_qkv = scatter_row(qkv_grad, 0)
            sums = spread(dpre, qkv, spot, block, ways, True)
            arrived = send_pairs(sums, ways)
            sums, flown = covered(sums, out_flying)
            own, pairs = add_pairs(sums, arrived)
            late_resids = after(resids, arrays_of(pairs))
            outputs = [
                (resid + out.astype(F32)).astype(BF)
                for resid, out in zip(late_resids[:-1], ffn_outs)
            ] + [(late_resids[-1] + total_of(out_own, flown)).astype(BF)]
            arrived = scatter_cols(pairs, ways, "split")
            dconv, dgain, gain_two_grad = after(
                (dconv, dgain, gain_two_grad), arrays_of(pairs)
            )
            conv_sum = dconv.reshape(4, 8, 3, hw).sum(axis=1).transpose(1, 2, 0)
            early = sum_over(
                jnp.concatenate(
                    [conv_sum.reshape(-1), jnp.sum(dgain, axis=0), gain_two_grad]
                ),
                "row", rows_ways,
            )
            firsts[0] = after(firsts[0][0], arrays_of(pairs)), firsts[0][1]
            stat, early = after((stat, early), arrays_of(pairs))
            means.append(sum_cols(stat.reshape(tokens, 128)[:, 0], ways)[:, None] / width)
            head_sum = sum_cols(early[12 * hw : 12 * hw + 128], ways)
    conv_grads = lax.dynamic_slice_in_dim(
        early[: 12 * hw].reshape(3, hw, 4), row * share, share, axis=1
    )
    grad_two = lax.dynamic_slice_in_dim(early[12 * hw + 128 :], row * share, share)
    output, conv_grads, grad_two = lax.optimization_barrier(
        (jnp.stack(outputs), [conv_grads[kind] for kind in range(3)], grad_two)
    )
    firsts.append((own, pieces_after(arrived, output, conv_grads, grad_two)))
    input_grads, gain_one_grad = [], 0.0
    for m in range(micro):
        act_grad = total_of(*firsts[m])
        unit = inputs[m].astype(F32) * inv_ones[m]
        gain_one_grad = gain_one_grad + jnp.sum(act_grad * unit, axis=0)
        input_grads.append(
            resid_grads[m] + inv_ones[m] * (act_grad * own_one - unit * means[m])
        )

    grad_qkv, grad_out, grad_gate, grad_up, grad_down = (
        grad.astype(F32) for grad in (grad_qkv, grad_out, grad_gate, grad_up, grad_down)
    )
    late = sum_over(gain_one_grad, "row", rows_ways)
    grad_head = lax.dynamic_slice_in_dim(
        head_sum, row * head_gain.shape[0], head_gain.shape[0]
    )
    grad_one = lax.dynamic_slice_in_dim(late, row * share, share)
    return (
        output,
        jnp.stack(input_grads),
        grad_one,
        grad_qkv[:, :hw],
        grad_qkv[:, hw : 2 * hw],
        grad_qkv[:, 2 * hw : 3 * hw],
        grad_qkv[:, 3 * hw : 3 * hw + heads],
        conv_grads[0],
        conv_grads[1],
        conv_grads[2],
        grad_head,
        grad_out,
        grad_two,
        grad_gate.T,
        grad_up.T,
        grad_down,
    )


def solution(mesh):
    both = P(("col", "row"))
    taps = P(("col", "row"), None)
    rows_cols, cols_rows = P("row", "col"), P("col", "row")
    tokens = P(None, "row", "col")
    in_specs = (
        tokens, tokens, P(None, "row"), both, rows_cols, rows_cols, rows_cols, rows_cols,
        taps, taps, taps, P("row"), cols_rows, both, rows_cols, rows_cols, cols_rows,
    )
    out_specs = (
        tokens, tokens, both, rows_cols, rows_cols, rows_cols, rows_cols,
        taps, taps, taps, P("row"), cols_rows, both, rows_cols, rows_cols, cols_rows,
    )
    body = partial(local, mesh.shape["col"], mesh.shape["row"])
    return jax.shard_map(body, mesh=mesh, in_specs=in_specs, out_specs=out_specs, check_vma=False)
```
